256 devices in a mesh: grid: 16 (over y_hi, z), dom: 16 (over y_lo, x, core).
Axes of the slice: x: 4, y: 4 (y_hi: 2, y_lo: 2; y = y_hi * 2 + y_lo), z: 8, core: 2. Of those that a mesh axis runs over, the one named last changes fastest.
Arguments:
- fields: float32 [16, 64, 16, 16, 256], P('grid', 'dom'), may hold values from -6 to 6
- cutoffs: int32 [16, 4], P('grid'), may hold values from 0 to 2
- weights: int32 [16], P('grid'), may hold values from -3 to 3, as said below
- diffusion: float32 [4], replicated, may hold values from 0.03 to 0.12
- courant: float32 [4], replicated, may hold values from -0.2 to 0.2
Outputs:
- combined_fields: float32 [16, 64, 16, 16, 256], P('grid', 'dom')
The draws below stay inside these ranges and needn't reach their ends.
Inputs may be any that keep to these rules, and one draw needn't show every extreme that they name: `weights`: each weight is a nonzero integer of magnitude 1 to 3.
All inputs are finite; a program needn't handle non-finite values.
Results may differ from the reference program's by a relative error of at most 0.0003.
Values sent between devices are 32-bit elements; how exact they have to be, the bound alone decides.
A program may use at most 64 MiB of HBM per device.

```python
import jax
import jax.numpy as jnp
from jax import lax

N2 = 16
N3 = 16
N4 = 256
STEPS = 2
N1 = 64
GRIDS = 16


def draw_weights(key, part):
    magnitude = jax.random.randint(jax.random.fold_in(key, 11), (GRIDS,), 1, 4, dtype=jnp.int32)
    sign_bits = jax.random.randint(jax.random.fold_in(key, 23), (GRIDS,), 0, 2, dtype=jnp.int32)
    return magnitude * (2 * sign_bits - 1)


def place_ends(entries, rng, least, largest):
    dims = entries.shape
    place = [jax.random.randint(jax.random.fold_in(rng, axis), (), 0, dims[axis]) for axis in range(len(dims))]
    entries = entries.at[tuple(place)].set(least)
    longest = dims.index(max(dims))
    place[longest] = (place[longest] + 1) % dims[longest]
    return entries.at[tuple(place)].set(largest)


def shard_levels(stream_key, shape, pieces, smallest, top_value):
    level = 1.0
    for dim, shards_of in pieces:
        draws = jax.random.uniform(jax.random.fold_in(jax.random.fold_in(stream_key, 6), dim), (shards_of,), jnp.float32, smallest / len(pieces), top_value / len(pieces))
        level = level * jnp.repeat(jnp.exp(draws), shape[dim] // shards_of).reshape((-1,) + (1,) * (len(shape) - 1 - dim))
    return level


def centred(own_key, extent, spread, most, shards=(), kind=jnp.bfloat16):
    level = shard_levels(own_key, extent, shards, -0.22, 0.18) if shards else 1.0
    values = jax.random.normal(own_key, extent, jnp.float32) * spread * level
    return jnp.minimum(jnp.maximum(values, -most), most).astype(kind)


def setup_inputs(seed: int = 0) -> dict:
    arg_keys = jax.random.split(jax.random.key(seed), 6)
    fields = centred(arg_keys[0], (GRIDS, N1, N2, N3, N4), 1.0, 6.0, ((0, 16), (1, 16)), jnp.float32)
    cutoffs = place_ends(jax.random.randint(arg_keys[1], (GRIDS, 4), 0, 3), jax.random.fold_in(arg_keys[1], 1), 0, 2).astype(jnp.int32)
    weights = draw_weights(jax.random.fold_in(arg_keys[5], 71), 0)
    diffusion = jnp.clip(jax.random.uniform(arg_keys[3], (4,), jnp.float32, 0.03, 0.12), 0.03, 0.12)
    courant = jnp.clip(jax.random.uniform(arg_keys[4], (4,), jnp.float32, -0.2, 0.2), -0.2, 0.2)
    return {"fields": fields, "cutoffs": cutoffs, "weights": weights, "diffusion": diffusion, "courant": courant}


def neighbours(length):
    positions = jnp.arange(length, dtype=jnp.int32)
    spacing = jnp.bitwise_and(positions, -positions)
    left_at = jnp.remainder(positions - spacing, length).astype(jnp.int32)
    right_at = jnp.remainder(positions + spacing, length).astype(jnp.int32)
    return positions, spacing, left_at, right_at


def shaped(vector, axis_at, order_of):
    dims_list = [1] * order_of
    dims_list[axis_at] = vector.shape[0]
    return vector.reshape(dims_list)


def hierarchize(values, axis_at):
    length = values.shape[axis_at]
    positions, spacing, left_at, right_at = neighbours(length)
    factor = shaped(jnp.where(positions > 0, 0.5, 0.0).astype(jnp.float32), axis_at, values.ndim)
    return values - factor * (jnp.take(values, left_at, axis=axis_at) + jnp.take(values, right_at, axis=axis_at))


def dehierarchize(values, axis_at):
    length = values.shape[axis_at]
    positions, spacing, left_at, right_at = neighbours(length)
    for level_bit in reversed(range(length.bit_length() - 1)):
        factor = shaped(jnp.where(spacing == 2 ** level_bit, 0.5, 0.0).astype(jnp.float32), axis_at, values.ndim)
        values = values + factor * (jnp.take(values, left_at, axis=axis_at) + jnp.take(values, right_at, axis=axis_at))
    return values


def tendency(centre, neighbour_pairs, diffusion, courant):
    result = jnp.zeros_like(centre)
    for axis_at in range(4):
        forward, behind = neighbour_pairs[axis_at]
        result = result + diffusion[axis_at] * (forward - 2.0 * centre + behind) - courant[axis_at] * (forward - behind)
    return result


def rate_full(values, diffusion, courant):
    neighbour_pairs = [(jnp.roll(values, -1, axis_at), jnp.roll(values, 1, axis_at)) for axis_at in range(4)]
    return tendency(values, neighbour_pairs, diffusion, courant)


def kept_mask(cutoff_row, position_lists):
    kept_cells = jnp.ones((1, 1, 1, 1), jnp.float32)
    for axis_at in range(4):
        stride = jnp.left_shift(jnp.int32(1), cutoff_row[axis_at].astype(jnp.int32))
        divides = (jnp.remainder(position_lists[axis_at], stride) == 0).astype(jnp.float32)
        kept_cells = kept_cells * shaped(divides, axis_at, 4)
    return kept_cells


def reference(fields, cutoffs, weights, diffusion, courant):
    grid_shape = fields.shape[1:]
    position_lists = [jnp.arange(grid_shape[axis_at], dtype=jnp.int32) for axis_at in range(4)]

    def accumulate(running, operand):
        solution, cutoff_row, weight = operand
        for stepping in range(STEPS):
            section_one = solution + rate_full(solution, diffusion, courant)
            section_two = 0.75 * solution + 0.25 * (section_one + rate_full(section_one, diffusion, courant))
            solution = solution / 3.0 + (2.0 / 3.0) * (section_two + rate_full(section_two, diffusion, courant))
        for axis_at in range(4):
            solution = hierarchize(solution, axis_at)
        term = weight.astype(jnp.float32) * kept_mask(cutoff_row, position_lists) * solution
        return running + term, None

    summed, unused = lax.scan(accumulate, jnp.zeros(grid_shape, jnp.float32), (fields, cutoffs, weights))
    summed = summed / GRIDS

    def restore(cutoff_row):
        values = kept_mask(cutoff_row, position_lists) * summed
        for axis_at in range(4):
            values = dehierarchize(values, axis_at)
        return values

    return lax.map(restore, cutoffs)
```

```python
import functools
import math

import jax
import jax.numpy as jnp
from jax import lax
from jax.experimental import pallas as pl
from jax.experimental.pallas import tpu as pltpu
from jax.sharding import PartitionSpec as P

SERIES = (1.0, 2.0, 2.0, 4.0 / 3.0, 7.0 / 12.0, 1.0 / 6.0, 1.0 / 36.0)
DEGREE = 6
ROWS = 4
LOW = 6
HIGH = 7
WINDOW = LOW + ROWS + HIGH
RING = 8
MESH = pl.DeviceIdType.MESH
F32 = jnp.float32
BF16 = jnp.bfloat16


def split(x):
    hi = x.astype(BF16)
    return hi, (x - hi.astype(F32)).astype(BF16)


def dot(a, b):
    return jnp.dot(a, b, preferred_element_type=F32)


def fine_surplus(to, source, n):
    ahead = (source - to) & (n - 1)
    near = (ahead == 1) | (ahead == n - 1)
    far = (ahead == 2) | (ahead == n - 2)
    half = ((to & 1) == 1) & near | ((to & 3) == 2) & far
    return jnp.where(ahead == 0, 1.0, jnp.where(half, -0.5, 0.0)).astype(F32)


def fine_restore(to, source, n):
    ahead = (source - to) & (n - 1)
    place = to & 3
    toward = jnp.where(place == 1, ahead, (n - ahead) & (n - 1))
    odd = jnp.where(
        toward == n - 1, 0.75, jnp.where(toward == 1, 0.5, jnp.where(toward == 3, 0.25, 0.0))
    )
    even = jnp.where((place == 2) & ((ahead == 2) | (ahead == n - 2)), 0.5, 0.0)
    return jnp.where(ahead == 0, 1.0, jnp.where((to & 1) == 1, odd, even)).astype(F32)


def coefficients(alpha, beta):
    up, down = [1.0], [1.0]
    for _ in range(DEGREE):
        up.append(up[-1] * alpha)
        down.append(down[-1] * beta)
    q = {}
    for m in range(DEGREE + 1):
        for j in range(m - DEGREE, DEGREE - m + 1):
            total = 0.0
            for l in range(abs(j), DEGREE - m + 1, 2):
                i = (l + j) // 2
                factor = SERIES[m + l] * math.comb(m + l, m) * math.comb(l, i)
                total = total + factor * up[i] * down[l - i]
            q[m, j] = total
    return q


def kernel(
    sizes,
    cutoffs, weights, diffusion, courant, fields, out,
    window, held_a, held_b, product, evolved, surplus, arrived, paired, combined,
    t_hi, t_lo, fine4, fine23, back4, back23, mask23,
    own_sem, low_send, low_recv, high_send, high_recv, plus_send, plus_recv, minus_send, minus_recv,
    pair_send, pair_recv, gplus_send, gplus_recv, gminus_send, gminus_recv, row_send, row_recv,
):
    n2, n3, n4 = sizes
    plane = n2 * n3
    part = ROWS * n2 // (2 * RING)
    half = ROWS * n2 // 2
    grid_at, dom_at = lax.axis_index("grid"), lax.axis_index("dom")
    doms = lax.axis_size("dom")
    above, below = lax.rem(dom_at + 1, doms), lax.rem(dom_at + doms - 1, doms)
    z = lax.rem(grid_at, RING)
    base = grid_at - z
    z_plus, z_minus = base + lax.rem(z + 1, RING), base + lax.rem(z + RING - 1, RING)
    partner = lax.rem(grid_at + RING, 2 * RING)

    barrier = pltpu.get_barrier_semaphore()
    for device in (
        (grid_at, above), (grid_at, below), (z_plus, dom_at), (z_minus, dom_at), (partner, dom_at),
    ):
        pl.semaphore_signal(barrier, inc=1, device_id=device, device_id_type=MESH)
    pl.semaphore_wait(barrier, 5)

    def send(source, target, device, send_sem, recv_sem):
        copy = pltpu.make_async_remote_copy(
            src_ref=source, dst_ref=target, send_sem=send_sem, recv_sem=recv_sem,
            device_id=device, device_id_type=MESH,
        )
        copy.start()
        return copy

    high, low = {}, {}
    for d in range(ROWS):
        high[d] = send(
            fields.at[0, d], window.at[LOW + ROWS + d], (grid_at, below), high_send.at[d], high_recv.at[d]
        )
        low[d] = send(
            fields.at[0, ROWS - 1 - d], window.at[LOW - 1 - d], (grid_at, above), low_send.at[d], low_recv.at[d]
        )
    own = pltpu.make_async_copy(fields.at[0], window.at[LOW : LOW + ROWS], own_sem)
    own.start()

    alpha = [diffusion[d] - courant[d] for d in range(4)]
    beta = [diffusion[d] + courant[d] for d in range(4)]
    centre = -2.0 * (diffusion[0] + diffusion[1] + diffusion[2] + diffusion[3])
    q = coefficients(alpha[0], beta[0])

    source4 = lax.broadcasted_iota(jnp.int32, (n4, n4), 0)
    to4 = lax.broadcasted_iota(jnp.int32, (n4, n4), 1)
    ahead4 = (source4 - to4) & (n4 - 1)
    t = jnp.where(
        ahead4 == 0, centre, jnp.where(ahead4 == 1, alpha[3], jnp.where(ahead4 == n4 - 1, beta[3], 0.0))
    )
    hi, lo = split(t)
    t_hi[...] = hi
    t_lo[...] = lo
    fine4[...] = fine_surplus(to4, source4, n4).astype(BF16)
    back4[...] = fine_restore(to4, source4, n4).astype(BF16)
    to = lax.broadcasted_iota(jnp.int32, (plane, plane), 0)
    source = lax.broadcasted_iota(jnp.int32, (plane, plane), 1)
    shift = n3.bit_length() - 1
    to2, to3, source2, source3 = to >> shift, to & (n3 - 1), source >> shift, source & (n3 - 1)
    fine23[...] = (fine_surplus(to2, source2, n2) * fine_surplus(to3, source3, n3)).astype(BF16)
    back23[...] = (fine_restore(to2, source2, n2) * fine_restore(to3, source3, n3)).astype(BF16)
    line = lax.broadcasted_iota(jnp.int32, (plane, n4), 0)
    cell = lax.broadcasted_iota(jnp.int32, (plane, n4), 1)
    stride = [jnp.left_shift(jnp.int32(1), cutoffs[0, d]) for d in range(4)]
    off = ((line >> shift) & (stride[1] - 1)) | (line & (n3 - 1) & (stride[2] - 1)) | (cell & (stride[3] - 1))
    mask23[...] = jnp.where(off == 0, 1.0, 0.0).astype(F32)
    kept_row = [jnp.where((r & (stride[0] - 1)) == 0, 1.0, 0.0).astype(F32) for r in range(ROWS)]
    weight = weights[0].astype(F32) * (1.0 / (2 * RING))

    own.wait()
    block = 4

    def wait_high(d):
        high[d].wait_recv()
        if d < HIGH - ROWS:
            high[ROWS + d] = send(
                window.at[LOW + ROWS + d], window.at[LOW + 2 * ROWS + d], (grid_at, below),
                high_send.at[ROWS + d], high_recv.at[ROWS + d],
            )

    def wait_low(d):
        low[d].wait_recv()
        if d < LOW - ROWS:
            low[ROWS + d] = send(
                window.at[LOW - 1 - d], window.at[LOW - 1 - ROWS - d], (grid_at, above),
                low_send.at[ROWS + d], low_recv.at[ROWS + d],
            )

    def level(m, now, then):
        def row(r, carry):
            if m < DEGREE:
                flat = now[r, 1 : n2 + 1].reshape(plane, n4)
                hi, lo = split(flat)
                product[...] = dot(hi, t_hi[...]) + dot(lo, t_hi[...]) + dot(hi, t_lo[...])
            for i in range(0, n2, block):
                total = None
                for j in range(m - DEGREE, DEGREE - m + 1):
                    term = q[m, j] * window[LOW + r + j, i : i + block]
                    total = term if total is None else total + term
                if m < DEGREE:
                    here = now[r, i + 1 : i + 1 + block]
                    total = total + product[i * n3 : (i + block) * n3].reshape(block, n3, n4)
                    total = total + alpha[1] * now[r, i + 2 : i + 2 + block] + beta[1] * now[r, i : i + block]
                    total = total + alpha[2] * pltpu.roll(here, n3 - 1, 1) + beta[2] * pltpu.roll(here, 1, 1)
                if m > 0:
                    then[r, i + 1 : i + 1 + block] = total
                else:
                    evolved[r, i : i + block] = total
            if m > 0:
                then[r, 0] = then[r, n2]
                then[r, n2 + 1] = then[r, 1]
            return carry

        lax.fori_loop(0, ROWS + 1, row, 0)

    now, then = held_a, held_b
    for m in range(DEGREE, -1, -1):
        d = DEGREE - m
        wait_high(d)
        if d > 0:
            wait_low(d - 1)
        level(m, now, then)
        now, then = then, now

    def surplus_of(r, flat):
        hi, lo = split(flat)
        flat = dot(hi, fine4[...]) + dot(lo, fine4[...])
        hi, lo = split(flat)
        flat = dot(fine23[...], hi) + dot(fine23[...], lo)
        flat = flat * (mask23[...] * (weight * kept_row[r]))
        surplus[r * n2 : (r + 1) * n2] = flat.reshape(n2, n3, n4)

    def evolved_row(r):
        return evolved[r].reshape(plane, n4)

    surplus_of(0, evolved_row(0))
    surplus_of(1, evolved_row(1) - 0.5 * (evolved_row(0) + evolved_row(2)))
    surplus_of(2, evolved_row(2) - 0.5 * (evolved_row(0) + evolved_row(4)))
    surplus_of(3, evolved_row(3) - 0.5 * (evolved_row(2) + evolved_row(4)))

    def piece(h, offset):
        return pl.ds(h * half + lax.rem(z + offset + RING, RING) * part, part)

    plus_order = [(0, 4), (1, 3), (0, 3), (1, 2), (0, 2), (1, 1), (0, 1)]
    minus_order = [(1 - h, -o) for h, o in plus_order]
    plus, minus = [], []
    for step in range(len(plus_order)):
        for order, copies, slot, device, send_sem, recv_sem in (
            (plus_order, plus, 0, z_plus, plus_send, plus_recv),
            (minus_order, minus, 1, z_minus, minus_send, minus_recv),
        ):
            where = piece(*order[step])
            if step >= 2:
                copies[step - 2].wait_recv()
                surplus[where] = surplus[where] + arrived[slot, step - 2]
            copies.append(
                send(surplus.at[where], arrived.at[slot, step], (device, dom_at), send_sem.at[step], recv_sem.at[step])
            )
    pair = []
    for h in range(2):
        plus[6 - h].wait_recv()
        minus[5 + h].wait_recv()
        mine = piece(h, 0)
        surplus[mine] = surplus[mine] + (arrived[0, 6 - h] + arrived[1, 5 + h])
        pair.append(send(surplus.at[mine], paired.at[h], (partner, dom_at), pair_send.at[h], pair_recv.at[h]))

    gplus_order = [(0, 0), (1, 0), (0, -1), (1, -1), (0, -2), (1, -2), (0, -3)]
    gminus_order = [(1 - h, -o) for h, o in gplus_order]
    gplus, gminus = [], []
    for h in range(2):
        pair[h].wait_recv()
        mine = piece(h, 0)
        combined[mine] = surplus[mine] + paired[h]
    for step in range(len(gplus_order)):
        for order, copies, device, send_sem, recv_sem in (
            (gplus_order, gplus, z_plus, gplus_send, gplus_recv),
            (gminus_order, gminus, z_minus, gminus_send, gminus_recv),
        ):
            if step >= 2:
                copies[step - 2].wait_recv()
            where = piece(*order[step])
            copies.append(
                send(combined.at[where], combined.at[where], (device, dom_at), send_sem.at[step], recv_sem.at[step])
            )
    for copies in (gplus, gminus):
        for step in (5, 6):
            copies[step].wait_recv()

    last = send(
        combined.at[0:n2], combined.at[ROWS * n2 : (ROWS + 1) * n2], (grid_at, below), row_send, row_recv
    )

    def masked(r):
        return combined[r * n2 : (r + 1) * n2].reshape(plane, n4) * mask23[...]

    def restore(r, flat):
        hi, lo = split(flat)
        flat = dot(hi, back4[...]) + dot(lo, back4[...])
        hi, lo = split(flat)
        flat = dot(back23[...], hi) + dot(back23[...], lo)
        out[0, r] = flat.reshape(n2, n3, n4)

    restore(0, masked(0))
    last.wait_recv()
    evolved[4] = masked(4).reshape(n2, n3, n4)
    evolved[2] = (kept_row[2] * masked(2) + 0.5 * (masked(0) + evolved_row(4))).reshape(n2, n3, n4)
    restore(2, evolved_row(2))
    restore(1, kept_row[1] * masked(1) + 0.5 * (masked(0) + evolved_row(2)))
    restore(3, kept_row[3] * masked(3) + 0.5 * (evolved_row(2) + evolved_row(4)))

    for copy in (*high.values(), *low.values(), *plus, *minus, *pair, *gplus, *gminus, last):
        copy.wait_send()


def shards(fields, cutoffs, weights, diffusion, courant):
    n2, n3, n4 = fields.shape[2:]
    plane = n2 * n3
    part = ROWS * n2 // (2 * RING)
    row = (n2, n3, n4)
    dma = pltpu.SemaphoreType.DMA
    return pl.pallas_call(
        functools.partial(kernel, row),
        out_shape=jax.ShapeDtypeStruct(fields.shape, F32),
        in_specs=[pl.BlockSpec(memory_space=pltpu.SMEM)] * 4 + [pl.BlockSpec(memory_space=pl.ANY)],
        out_specs=pl.BlockSpec(memory_space=pltpu.VMEM),
        scratch_shapes=[
            pltpu.VMEM((WINDOW, *row), F32),
            pltpu.VMEM((ROWS + 1, n2 + 2, n3, n4), F32),
            pltpu.VMEM((ROWS + 1, n2 + 2, n3, n4), F32),
            pltpu.VMEM((plane, n4), F32),
            pltpu.VMEM((ROWS + 1, *row), F32),
            pltpu.VMEM((ROWS * n2, n3, n4), F32),
            pltpu.VMEM((2, 7, part, n3, n4), F32),
            pltpu.VMEM((2, part, n3, n4), F32),
            pltpu.VMEM(((ROWS + 1) * n2, n3, n4), F32),
            pltpu.VMEM((n4, n4), BF16),
            pltpu.VMEM((n4, n4), BF16),
            pltpu.VMEM((n4, n4), BF16),
            pltpu.VMEM((plane, plane), BF16),
            pltpu.VMEM((n4, n4), BF16),
            pltpu.VMEM((plane, plane), BF16),
            pltpu.VMEM((plane, n4), F32),
            dma,
            dma((LOW,)), dma((LOW,)), dma((HIGH,)), dma((HIGH,)),
            dma((7,)), dma((7,)), dma((7,)), dma((7,)),
            dma((2,)), dma((2,)),
            dma((7,)), dma((7,)), dma((7,)), dma((7,)),
            dma, dma,
        ],
        compiler_params=pltpu.CompilerParams(
            collective_id=0, has_side_effects=True, vmem_limit_bytes=48 * 1024 * 1024
        ),
        name="advect_combine",
    )(cutoffs, weights, diffusion, courant, fields)


def solution(mesh):
    in_specs = (P("grid", "dom", None, None, None), P("grid", None), P("grid"), P(), P())
    out_specs = P("grid", "dom", None, None, None)
    return jax.shard_map(shards, mesh=mesh, in_specs=in_specs, out_specs=out_specs, check_vma=False)
```

```python
import functools
import math

import jax
import jax.numpy as jnp
from jax import lax
from jax.experimental import pallas as pl
from jax.experimental.pallas import tpu as pltpu
from jax.sharding import PartitionSpec as P

SERIES = (1.0, 2.0, 2.0, 4.0 / 3.0, 7.0 / 12.0, 1.0 / 6.0, 1.0 / 36.0)
DEGREE = 6
ROWS = 4
LOW = 6
HIGH = 7
WINDOW = LOW + ROWS + HIGH
RING = 8
MESH = pl.DeviceIdType.MESH
F32 = jnp.float32
BF16 = jnp.bfloat16


def split(x):
    hi = x.astype(BF16)
    return hi, (x - hi.astype(F32)).astype(BF16)


def dot(a, b):
    return jnp.dot(a, b, preferred_element_type=F32)


def fine_surplus(to, source, n):
    ahead = (source - to) & (n - 1)
    near = (ahead == 1) | (ahead == n - 1)
    far = (ahead == 2) | (ahead == n - 2)
    half = ((to & 1) == 1) & near | ((to & 3) == 2) & far
    return jnp.where(ahead == 0, 1.0, jnp.where(half, -0.5, 0.0)).astype(F32)


def fine_restore(to, source, n):
    ahead = (source - to) & (n - 1)
    place = to & 3
    toward = jnp.where(place == 1, ahead, (n - ahead) & (n - 1))
    odd = jnp.where(
        toward == n - 1, 0.75, jnp.where(toward == 1, 0.5, jnp.where(toward == 3, 0.25, 0.0))
    )
    even = jnp.where((place == 2) & ((ahead == 2) | (ahead == n - 2)), 0.5, 0.0)
    return jnp.where(ahead == 0, 1.0, jnp.where((to & 1) == 1, odd, even)).astype(F32)


def coefficients(alpha, beta):
    up, down = [1.0], [1.0]
    for _ in range(DEGREE):
        up.append(up[-1] * alpha)
        down.append(down[-1] * beta)
    q = {}
    for m in range(DEGREE + 1):
        for j in range(m - DEGREE, DEGREE - m + 1):
            total = 0.0
            for l in range(abs(j), DEGREE - m + 1, 2):
                i = (l + j) // 2
                factor = SERIES[m + l] * math.comb(m + l, m) * math.comb(l, i)
                total = total + factor * up[i] * down[l - i]
            q[m, j] = total
    return q


def kernel(
    sizes,
    cutoffs, weights, diffusion, courant, fields, out,
    window, held_a, held_b, product, evolved, surplus, arrived, paired, combined,
    t_hi, t_lo, fine4, fine23, back4, back23, mask23,
    own_sem, low_send, low_recv, high_send, high_recv, plus_send, plus_recv, minus_send, minus_recv,
    pair_send, pair_recv, gplus_send, gplus_recv, gminus_send, gminus_recv, row_send, row_recv,
):
    n2, n3, n4 = sizes
    plane = n2 * n3
    part = n2 // RING
    grid_at, dom_at = lax.axis_index("grid"), lax.axis_index("dom")
    doms = lax.axis_size("dom")
    above, below = lax.rem(dom_at + 1, doms), lax.rem(dom_at + doms - 1, doms)
    z = lax.rem(grid_at, RING)
    base = grid_at - z
    z_plus, z_minus = base + lax.rem(z + 1, RING), base + lax.rem(z + RING - 1, RING)
    partner = lax.rem(grid_at + RING, 2 * RING)

    barrier = pltpu.get_barrier_semaphore()
    for device in (
        (grid_at, above), (grid_at, below), (z_plus, dom_at), (z_minus, dom_at), (partner, dom_at),
    ):
        pl.semaphore_signal(barrier, inc=1, device_id=device, device_id_type=MESH)
    pl.semaphore_wait(barrier, 5)

    def send(source, target, device, send_sem, recv_sem):
        copy = pltpu.make_async_remote_copy(
            src_ref=source, dst_ref=target, send_sem=send_sem, recv_sem=recv_sem,
            device_id=device, device_id_type=MESH,
        )
        copy.start()
        return copy

    high, low = {}, {}
    for d in range(ROWS):
        high[d] = send(
            fields.at[0, d], window.at[LOW + ROWS + d], (grid_at, below), high_send.at[d], high_recv.at[d]
        )
        low[d] = send(
            fields.at[0, ROWS - 1 - d], window.at[LOW - 1 - d], (grid_at, above), low_send.at[d], low_recv.at[d]
        )
    own = pltpu.make_async_copy(fields.at[0], window.at[LOW : LOW + ROWS], own_sem)
    own.start()

    alpha = [diffusion[d] - courant[d] for d in range(4)]
    beta = [diffusion[d] + courant[d] for d in range(4)]
    centre = -2.0 * (diffusion[0] + diffusion[1] + diffusion[2] + diffusion[3])
    q = coefficients(alpha[0], beta[0])

    source4 = lax.broadcasted_iota(jnp.int32, (n4, n4), 0)
    to4 = lax.broadcasted_iota(jnp.int32, (n4, n4), 1)
    ahead4 = (source4 - to4) & (n4 - 1)
    t = jnp.where(
        ahead4 == 0, centre, jnp.where(ahead4 == 1, alpha[3], jnp.where(ahead4 == n4 - 1, beta[3], 0.0))
    )
    hi, lo = split(t)
    t_hi[...] = hi
    t_lo[...] = lo
    fine4[...] = fine_surplus(to4, source4, n4).astype(BF16)
    back4[...] = fine_restore(to4, source4, n4).astype(BF16)
    to = lax.broadcasted_iota(jnp.int32, (plane, plane), 0)
    source = lax.broadcasted_iota(jnp.int32, (plane, plane), 1)
    shift = n3.bit_length() - 1
    to2, to3, source2, source3 = to >> shift, to & (n3 - 1), source >> shift, source & (n3 - 1)
    fine23[...] = (fine_surplus(to2, source2, n2) * fine_surplus(to3, source3, n3)).astype(BF16)
    back23[...] = (fine_restore(to2, source2, n2) * fine_restore(to3, source3, n3)).astype(BF16)
    line = lax.broadcasted_iota(jnp.int32, (plane, n4), 0)
    cell = lax.broadcasted_iota(jnp.int32, (plane, n4), 1)
    stride = [jnp.left_shift(jnp.int32(1), cutoffs[0, d]) for d in range(4)]
    off = ((line >> shift) & (stride[1] - 1)) | (line & (n3 - 1) & (stride[2] - 1)) | (cell & (stride[3] - 1))
    mask23[...] = jnp.where(off == 0, 1.0, 0.0).astype(F32)
    kept_row = [jnp.where((r & (stride[0] - 1)) == 0, 1.0, 0.0).astype(F32) for r in range(ROWS)]
    weight = weights[0].astype(F32) * (1.0 / (2 * RING))

    own.wait()
    block = 4

    def wait_high(d):
        high[d].wait_recv()
        if d < HIGH - ROWS:
            high[ROWS + d] = send(
                window.at[LOW + ROWS + d], window.at[LOW + 2 * ROWS + d], (grid_at, below),
                high_send.at[ROWS + d], high_recv.at[ROWS + d],
            )

    def wait_low(d):
        low[d].wait_recv()
        if d < LOW - ROWS:
            low[ROWS + d] = send(
                window.at[LOW - 1 - d], window.at[LOW - 1 - ROWS - d], (grid_at, above),
                low_send.at[ROWS + d], low_recv.at[ROWS + d],
            )

    def level(d, first, stride, count):
        m = DEGREE - d
        now, then = (held_a, held_b) if d % 2 == 0 else (held_b, held_a)

        def row(index, carry):
            r = first + index * stride
            if d > 0:
                hi, lo = split(now[r, 1 : n2 + 1].reshape(plane, n4))
                product[...] = dot(hi, t_hi[...]) + dot(lo, t_hi[...]) + dot(hi, t_lo[...])
            for i in range(0, n2, block):
                total = None
                for j in range(-d, d + 1):
                    term = q[m, j] * window[LOW + r + j, i : i + block]
                    total = term if total is None else total + term
                if d > 0:
                    here = now[r, i + 1 : i + 1 + block]
                    total = total + product[i * n3 : (i + block) * n3].reshape(block, n3, n4)
                    total = total + alpha[1] * now[r, i + 2 : i + 2 + block] + beta[1] * now[r, i : i + block]
                    total = total + alpha[2] * pltpu.roll(here, n3 - 1, 1) + beta[2] * pltpu.roll(here, 1, 1)
                if m > 0:
                    then[r, i + 1 : i + 1 + block] = total
                else:
                    evolved[r, i : i + block] = total
            if m > 0:
                then[r, 0] = then[r, n2]
                then[r, n2 + 1] = then[r, 1]
            return carry

        if count == 1:
            row(0, 0)
        else:
            lax.fori_loop(0, count, row, 0)

    level(0, 1, 1, 2)
    for d in range(DEGREE):
        level(d, 0, 3, 2)
        level(d + 1, 1, 1, 2)
        if d > 0:
            level(d - 1, 4, 1, 1)
        wait_high(d)
        wait_low(d)
    level(DEGREE, 0, 3, 2)

    def surplus_of(r, flat):
        hi, lo = split(flat)
        flat = dot(hi, fine4[...]) + dot(lo, fine4[...])
        hi, lo = split(flat)
        flat = dot(fine23[...], hi) + dot(fine23[...], lo)
        flat = flat * (mask23[...] * (weight * kept_row[r]))
        surplus[r * n2 : (r + 1) * n2] = flat.reshape(n2, n3, n4)

    def evolved_row(r):
        return evolved[r].reshape(plane, n4)

    def piece(c, h, offset):
        return pl.ds((2 * c + h) * n2 + lax.rem(z + offset + RING, RING) * part, part)

    plus_order = [(0, 4), (1, 3), (0, 3), (1, 2), (0, 2), (1, 1), (0, 1)]
    minus_order = [(1 - h, -o) for h, o in plus_order]
    gplus_order = [(0, 0), (1, 0), (0, -1), (1, -1), (0, -2), (1, -2), (0, -3)]
    gminus_order = [(1 - h, -o) for h, o in gplus_order]
    steps = len(plus_order)
    plus, minus, gplus, gminus = [[], []], [[], []], [[], []], [[], []]
    pair, shifted = [[], []], []

    def scatter_round(c, pace):
        for step in range(2 * pace, min(2 * pace + 2, steps)):
            for order, copies, slot, device, send_sem, recv_sem in (
                (plus_order, plus[c], 0, z_plus, plus_send, plus_recv),
                (minus_order, minus[c], 1, z_minus, minus_send, minus_recv),
            ):
                where = piece(c, *order[step])
                if step >= 2:
                    copies[step - 2].wait_recv()
                    surplus[where] = surplus[where] + arrived[c, slot, step - 2]
                copies.append(
                    send(
                        surplus.at[where], arrived.at[c, slot, step], (device, dom_at),
                        send_sem.at[c, step], recv_sem.at[c, step],
                    )
                )

    def pair_round(c):
        for h in range(2):
            plus[c][6 - h].wait_recv()
            minus[c][5 + h].wait_recv()
            mine = piece(c, h, 0)
            surplus[mine] = surplus[mine] + (arrived[c, 0, 6 - h] + arrived[c, 1, 5 + h])
            pair[c].append(
                send(surplus.at[mine], paired.at[c, h], (partner, dom_at), pair_send.at[c, h], pair_recv.at[c, h])
            )

    def shift_row(offset):
        index = len(shifted)
        where = piece(0, 0, offset)
        target = pl.ds(ROWS * n2 + lax.rem(z + offset + RING, RING) * part, part)
        shifted.append(
            send(combined.at[where], combined.at[target], (grid_at, below), row_send.at[index], row_recv.at[index])
        )

    def landed(c, copies, order, step, sign):
        copies[step].wait_recv()
        h, offset = order[step]
        if c == 0 and h == 0:
            shift_row(offset - sign)

    def gather_round(c, pace):
        if pace == 0:
            for h in range(2):
                pair[c][h].wait_recv()
                mine = piece(c, h, 0)
                combined[mine] = surplus[mine] + paired[c, h]
        for step in range(2 * pace, min(2 * pace + 2, steps)):
            for order, copies, device, send_sem, recv_sem, sign in (
                (gplus_order, gplus[c], z_plus, gplus_send, gplus_recv, 1),
                (gminus_order, gminus[c], z_minus, gminus_send, gminus_recv, -1),
            ):
                if step >= 2:
                    landed(c, copies, order, step - 2, sign)
                where = piece(c, *order[step])
                copies.append(
                    send(
                        combined.at[where], combined.at[where], (device, dom_at),
                        send_sem.at[c, step], recv_sem.at[c, step],
                    )
                )
        if pace == 0 and c == 0:
            shift_row(0)

    def gather_end(c):
        for step in (5, 6):
            landed(c, gplus[c], gplus_order, step, 1)
            landed(c, gminus[c], gminus_order, step, -1)

    surplus_of(0, evolved_row(0))
    surplus_of(1, evolved_row(1) - 0.5 * (evolved_row(0) + evolved_row(2)))
    scatter_round(0, 0)
    level(DEGREE - 1, 4, 1, 1)
    wait_high(DEGREE)
    level(DEGREE, 4, 1, 1)
    surplus_of(2, evolved_row(2) - 0.5 * (evolved_row(0) + evolved_row(4)))
    surplus_of(3, evolved_row(3) - 0.5 * (evolved_row(2) + evolved_row(4)))
    scatter_round(1, 0)
    for pace in range(1, 4):
        for c in range(2):
            scatter_round(c, pace)
    for c in range(2):
        pair_round(c)
    for pace in range(4):
        for c in range(2):
            gather_round(c, pace)
    gather_end(0)

    def masked(r):
        return combined[r * n2 : (r + 1) * n2].reshape(plane, n4) * mask23[...]

    def restore(r, flat):
        hi, lo = split(flat)
        flat = dot(hi, back4[...]) + dot(lo, back4[...])
        hi, lo = split(flat)
        flat = dot(back23[...], hi) + dot(back23[...], lo)
        out[0, r] = flat.reshape(n2, n3, n4)

    restore(0, masked(0))
    gather_end(1)
    for copy in shifted:
        copy.wait_recv()
    evolved[4] = masked(4).reshape(n2, n3, n4)
    evolved[2] = (kept_row[2] * masked(2) + 0.5 * (masked(0) + evolved_row(4))).reshape(n2, n3, n4)
    restore(2, evolved_row(2))
    restore(1, kept_row[1] * masked(1) + 0.5 * (masked(0) + evolved_row(2)))
    restore(3, kept_row[3] * masked(3) + 0.5 * (evolved_row(2) + evolved_row(4)))

    rings = [copy for copies in (plus, minus, pair, gplus, gminus) for chunk in copies for copy in chunk]
    for copy in (*high.values(), *low.values(), *rings, *shifted):
        copy.wait_send()


def shards(fields, cutoffs, weights, diffusion, courant):
    n2, n3, n4 = fields.shape[2:]
    plane = n2 * n3
    part = n2 // RING
    row = (n2, n3, n4)
    dma = pltpu.SemaphoreType.DMA
    return pl.pallas_call(
        functools.partial(kernel, row),
        out_shape=jax.ShapeDtypeStruct(fields.shape, F32),
        in_specs=[pl.BlockSpec(memory_space=pltpu.SMEM)] * 4 + [pl.BlockSpec(memory_space=pl.ANY)],
        out_specs=pl.BlockSpec(memory_space=pltpu.VMEM),
        scratch_shapes=[
            pltpu.VMEM((WINDOW, *row), F32),
            pltpu.VMEM((ROWS + 1, n2 + 2, n3, n4), F32),
            pltpu.VMEM((ROWS + 1, n2 + 2, n3, n4), F32),
            pltpu.VMEM((plane, n4), F32),
            pltpu.VMEM((ROWS + 1, *row), F32),
            pltpu.VMEM((ROWS * n2, n3, n4), F32),
            pltpu.VMEM((2, 2, 7, part, n3, n4), F32),
            pltpu.VMEM((2, 2, part, n3, n4), F32),
            pltpu.VMEM(((ROWS + 1) * n2, n3, n4), F32),
            pltpu.VMEM((n4, n4), BF16),
            pltpu.VMEM((n4, n4), BF16),
            pltpu.VMEM((n4, n4), BF16),
            pltpu.VMEM((plane, plane), BF16),
            pltpu.VMEM((n4, n4), BF16),
            pltpu.VMEM((plane, plane), BF16),
            pltpu.VMEM((plane, n4), F32),
            dma,
            dma((LOW,)), dma((LOW,)), dma((HIGH,)), dma((HIGH,)),
            dma((2, 7)), dma((2, 7)), dma((2, 7)), dma((2, 7)),
            dma((2, 2)), dma((2, 2)),
            dma((2, 7)), dma((2, 7)), dma((2, 7)), dma((2, 7)),
            dma((8,)), dma((8,)),
        ],
        compiler_params=pltpu.CompilerParams(
            collective_id=0, has_side_effects=True, vmem_limit_bytes=60 * 1024 * 1024
        ),
        name="advect_combine",
    )(cutoffs, weights, diffusion, courant, fields)


def solution(mesh):
    in_specs = (P("grid", "dom", None, None, None), P("grid", None), P("grid"), P(), P())
    out_specs = P("grid", "dom", None, None, None)
    return jax.shard_map(shards, mesh=mesh, in_specs=in_specs, out_specs=out_specs, check_vma=False)
```

```python
import functools
import math

import jax
import jax.numpy as jnp
from jax import lax
from jax.experimental import pallas as pl
from jax.experimental.pallas import tpu as pltpu
from jax.sharding import PartitionSpec as P

SERIES = (1.0, 2.0, 2.0, 4.0 / 3.0, 7.0 / 12.0, 1.0 / 6.0, 1.0 / 36.0)
DEGREE = 6
ROWS = 4
LOW = 6
HIGH = 7
WINDOW = LOW + ROWS + HIGH
RING = 8
MESH = pl.DeviceIdType.MESH
F32 = jnp.float32
BF16 = jnp.bfloat16


def split(x):
    hi = x.astype(BF16)
    return hi, (x - hi.astype(F32)).astype(BF16)


def dot(a, b):
    return jnp.dot(a, b, preferred_element_type=F32)


def fine_surplus(to, source, n):
    ahead = (source - to) & (n - 1)
    near = (ahead == 1) | (ahead == n - 1)
    far = (ahead == 2) | (ahead == n - 2)
    half = ((to & 1) == 1) & near | ((to & 3) == 2) & far
    return jnp.where(ahead == 0, 1.0, jnp.where(half, -0.5, 0.0)).astype(F32)


def fine_restore(to, source, n):
    ahead = (source - to) & (n - 1)
    place = to & 3
    toward = jnp.where(place == 1, ahead, (n - ahead) & (n - 1))
    odd = jnp.where(
        toward == n - 1, 0.75, jnp.where(toward == 1, 0.5, jnp.where(toward == 3, 0.25, 0.0))
    )
    even = jnp.where((place == 2) & ((ahead == 2) | (ahead == n - 2)), 0.5, 0.0)
    return jnp.where(ahead == 0, 1.0, jnp.where((to & 1) == 1, odd, even)).astype(F32)


def coefficients(alpha, beta):
    up, down = [1.0], [1.0]
    for _ in range(DEGREE):
        up.append(up[-1] * alpha)
        down.append(down[-1] * beta)
    q = {}
    for m in range(DEGREE + 1):
        for j in range(m - DEGREE, DEGREE - m + 1):
            total = 0.0
            for l in range(abs(j), DEGREE - m + 1, 2):
                i = (l + j) // 2
                factor = SERIES[m + l] * math.comb(m + l, m) * math.comb(l, i)
                total = total + factor * up[i] * down[l - i]
            q[m, j] = total
    return q


def kernel(
    sizes,
    cutoffs, weights, diffusion, courant, fields, out,
    window, held_a, held_b, product, evolved, surplus, arrived, last, paired, combined,
    t_hi, t_lo, fine4, fine23, back4, back23, mask23,
    own_sem, low_send, low_recv, high_send, high_recv,
    ring_send, ring_recv, last_send, last_recv, pair_send, pair_recv,
    first_send, first_recv, gpair_send, gpair_recv, gring_send, gring_recv, row_send, row_recv,
):
    n2, n3, n4 = sizes
    plane = n2 * n3
    part = n2 // RING
    grid_at, dom_at = lax.axis_index("grid"), lax.axis_index("dom")
    doms = lax.axis_size("dom")
    above, below = lax.rem(dom_at + 1, doms), lax.rem(dom_at + doms - 1, doms)
    z = lax.rem(grid_at, RING)
    base = grid_at - z
    other = lax.rem(base + RING, 2 * RING)
    z_next = (lax.rem(z + 1, RING), lax.rem(z + RING - 1, RING))
    beside = [((base + at, dom_at), (other + at, dom_at)) for at in z_next]
    partner = (other + z, dom_at)
    y = base // RING
    y_other = 1 - y

    barrier = pltpu.get_barrier_semaphore()
    for device in ((grid_at, above), (grid_at, below), *beside[0], *beside[1], partner):
        pl.semaphore_signal(barrier, inc=1, device_id=device, device_id_type=MESH)
    own = pltpu.make_async_copy(fields.at[0], window.at[LOW : LOW + ROWS], own_sem)
    own.start()
    pl.semaphore_wait(barrier, 7)

    def send(source, target, device, send_sem, recv_sem):
        copy = pltpu.make_async_remote_copy(
            src_ref=source, dst_ref=target, send_sem=send_sem, recv_sem=recv_sem,
            device_id=device, device_id_type=MESH,
        )
        copy.start()
        return copy

    high, low = {}, {}
    for d in range(ROWS):
        high[d] = send(
            fields.at[0, d], window.at[LOW + ROWS + d], (grid_at, below), high_send.at[d], high_recv.at[d]
        )
        low[d] = send(
            fields.at[0, ROWS - 1 - d], window.at[LOW - 1 - d], (grid_at, above), low_send.at[d], low_recv.at[d]
        )
    alpha = [diffusion[d] - courant[d] for d in range(4)]
    beta = [diffusion[d] + courant[d] for d in range(4)]
    centre = -2.0 * (diffusion[0] + diffusion[1] + diffusion[2] + diffusion[3])
    q = coefficients(alpha[0], beta[0])

    source4 = lax.broadcasted_iota(jnp.int32, (n4, n4), 0)
    to4 = lax.broadcasted_iota(jnp.int32, (n4, n4), 1)
    ahead4 = (source4 - to4) & (n4 - 1)
    t = jnp.where(
        ahead4 == 0, centre, jnp.where(ahead4 == 1, alpha[3], jnp.where(ahead4 == n4 - 1, beta[3], 0.0))
    )
    hi, lo = split(t)
    t_hi[...] = hi
    t_lo[...] = lo
    fine4[...] = fine_surplus(to4, source4, n4).astype(BF16)
    back4[...] = fine_restore(to4, source4, n4).astype(BF16)
    to = lax.broadcasted_iota(jnp.int32, (plane, plane), 0)
    source = lax.broadcasted_iota(jnp.int32, (plane, plane), 1)
    shift = n3.bit_length() - 1
    to2, to3, source2, source3 = to >> shift, to & (n3 - 1), source >> shift, source & (n3 - 1)
    fine23[...] = (fine_surplus(to2, source2, n2) * fine_surplus(to3, source3, n3)).astype(BF16)
    back23[...] = (fine_restore(to2, source2, n2) * fine_restore(to3, source3, n3)).astype(BF16)
    line = lax.broadcasted_iota(jnp.int32, (plane, n4), 0)
    cell = lax.broadcasted_iota(jnp.int32, (plane, n4), 1)
    stride = [jnp.left_shift(jnp.int32(1), cutoffs[0, d]) for d in range(4)]
    off = ((line >> shift) & (stride[1] - 1)) | (line & (n3 - 1) & (stride[2] - 1)) | (cell & (stride[3] - 1))
    mask23[...] = jnp.where(off == 0, 1.0, 0.0).astype(F32)
    kept_row = [jnp.where((r & (stride[0] - 1)) == 0, 1.0, 0.0).astype(F32) for r in range(ROWS)]
    weight = weights[0].astype(F32) * (1.0 / (2 * RING))

    own.wait()
    block = 4

    def wait_high(d):
        high[d].wait_recv()
        if d < HIGH - ROWS:
            high[ROWS + d] = send(
                window.at[LOW + ROWS + d], window.at[LOW + 2 * ROWS + d], (grid_at, below),
                high_send.at[ROWS + d], high_recv.at[ROWS + d],
            )

    def wait_low(d):
        low[d].wait_recv()
        if d < LOW - ROWS:
            low[ROWS + d] = send(
                window.at[LOW - 1 - d], window.at[LOW - 1 - ROWS - d], (grid_at, above),
                low_send.at[ROWS + d], low_recv.at[ROWS + d],
            )

    def level(d, first, stride, count):
        m = DEGREE - d
        now, then = (held_a, held_b) if d % 2 == 0 else (held_b, held_a)

        def row(index, carry):
            r = first + index * stride
            if d > 0:
                hi, lo = split(now[r, 1 : n2 + 1].reshape(plane, n4))
                product[...] = dot(hi, t_hi[...]) + dot(lo, t_hi[...]) + dot(hi, t_lo[...])
            for i in range(0, n2, block):
                total = None
                for j in range(-d, d + 1):
                    term = q[m, j] * window[LOW + r + j, i : i + block]
                    total = term if total is None else total + term
                if d > 0:
                    here = now[r, i + 1 : i + 1 + block]
                    total = total + product[i * n3 : (i + block) * n3].reshape(block, n3, n4)
                    total = total + alpha[1] * now[r, i + 2 : i + 2 + block] + beta[1] * now[r, i : i + block]
                    total = total + alpha[2] * pltpu.roll(here, n3 - 1, 1) + beta[2] * pltpu.roll(here, 1, 1)
                if m > 0:
                    then[r, i + 1 : i + 1 + block] = total
                else:
                    evolved[r, i : i + block] = total
            if m > 0:
                then[r, 0] = then[r, n2]
                then[r, n2 + 1] = then[r, 1]
            return carry

        if count == 1:
            row(0, 0)
        else:
            lax.fori_loop(0, count, row, 0)

    level(0, 1, 1, 2)
    for d in range(DEGREE):
        level(d, 0, 3, 2)
        level(d + 1, 1, 1, 2)
        if d > 0:
            level(d - 1, 4, 1, 1)
        wait_high(d)
        wait_low(d)
    level(DEGREE, 0, 3, 2)

    def surplus_of(r, flat):
        hi, lo = split(flat)
        flat = dot(hi, fine4[...]) + dot(lo, fine4[...])
        hi, lo = split(flat)
        flat = dot(fine23[...], hi) + dot(fine23[...], lo)
        flat = flat * (mask23[...] * (weight * kept_row[r]))
        surplus[r * n2 : (r + 1) * n2] = flat.reshape(n2, n3, n4)

    def evolved_row(r):
        return evolved[r].reshape(plane, n4)

    def piece(c, h, offset):
        return pl.ds((2 * c + h) * n2 + lax.rem(z + offset + RING, RING) * part, part)

    def layer(c, h, offset, at):
        return pl.ds((2 * c + h) * n2 + lax.rem(z + offset + RING, RING) * part + at, 1)

    order = [[(0, 4), (1, 3), (0, 3), (1, 2), (0, 2), (1, 1), (0, 1)]]
    order.append([(1 - h, -o) for h, o in order[0]])
    gorder = [[(0, 0), (1, 0), (0, -1), (1, -1), (0, -2), (1, -2), (0, -3)]]
    gorder.append([(1 - h, -o) for h, o in gorder[0]])
    steps, inner = len(order[0]), len(order[0]) - 2
    ring, ends, pairs, first, gpairs, gring, shifted = {}, {}, {}, {}, {}, {}, []

    def scatter_round(c, pace):
        for step in range(2 * pace, min(2 * pace + 2, steps)):
            for way in range(2):
                h, offset = order[way][step]
                where = piece(c, h, offset)
                if step >= 2:
                    ring[c, way, step - 2].wait_recv()
                    surplus[where] = surplus[where] + arrived[c, way, step - 2]
                if step < inner:
                    ring[c, way, step] = send(
                        surplus.at[where], arrived.at[c, way, step], beside[way][0],
                        ring_send.at[c, way, step], ring_recv.at[c, way, step],
                    )
                    continue
                for across, at in ((1, y_other), (0, y)):
                    ends[c, way, h, across] = send(
                        surplus.at[layer(c, h, offset, at)], last.at[c, way, h, across], beside[way][across],
                        last_send.at[c, way, h, across], last_recv.at[c, way, h, across],
                    )
        if pace == 0:
            for h in range(2):
                pairs[c, h] = send(
                    surplus.at[layer(c, h, 0, y_other)], paired.at[c, h], partner,
                    pair_send.at[c, h], pair_recv.at[c, h],
                )

    def finish(c, h):
        pairs[c, h].wait_recv()
        mine = layer(c, h, 0, y)
        total = surplus[mine] + paired[c, h]
        for across in range(2):
            for way in range(2):
                ends[c, way, h, across].wait_recv()
            total = total + (last[c, 0, h, across] + last[c, 1, h, across])
        combined[mine] = total

    def shift_row(offset):
        index = len(shifted)
        where = piece(0, 0, offset)
        target = pl.ds(ROWS * n2 + lax.rem(z + offset + RING, RING) * part, part)
        shifted.append(
            send(combined.at[where], combined.at[target], (grid_at, below), row_send.at[index], row_recv.at[index])
        )

    def landed(c, way, step):
        h, offset = gorder[way][step]
        if step < 2:
            for across in range(2):
                first[c, way, h, across].wait_recv()
        else:
            gring[c, way, step - 2].wait_recv()
        if c == 0 and h == 0:
            shift_row(offset - (1 - 2 * way))

    def gather_round(c, pace):
        if pace == 0:
            for h in range(2):
                finish(c, h)
                mine = combined.at[layer(c, h, 0, y)]
                for across in (1, 0):
                    for way in range(2):
                        first[c, way, h, across] = send(
                            mine, mine, beside[way][across],
                            first_send.at[c, way, h, across], first_recv.at[c, way, h, across],
                        )
                gpairs[c, h] = send(mine, mine, partner, gpair_send.at[c, h], gpair_recv.at[c, h])
            return
        for step in range(2 * pace, min(2 * pace + 2, steps)):
            for way in range(2):
                landed(c, way, step - 2)
                where = combined.at[piece(c, *gorder[way][step])]
                gring[c, way, step - 2] = send(
                    where, where, beside[way][0], gring_send.at[c, way, step - 2], gring_recv.at[c, way, step - 2]
                )
        if pace == 1:
            for h in range(2):
                gpairs[c, h].wait_recv()
            if c == 0:
                shift_row(0)

    def gather_end(c):
        for step in (inner, inner + 1):
            for way in range(2):
                landed(c, way, step)

    surplus_of(0, evolved_row(0))
    surplus_of(1, evolved_row(1) - 0.5 * (evolved_row(0) + evolved_row(2)))
    scatter_round(0, 0)
    level(DEGREE - 1, 4, 1, 1)
    wait_high(DEGREE)
    level(DEGREE, 4, 1, 1)
    surplus_of(2, evolved_row(2) - 0.5 * (evolved_row(0) + evolved_row(4)))
    surplus_of(3, evolved_row(3) - 0.5 * (evolved_row(2) + evolved_row(4)))
    scatter_round(1, 0)
    for pace in range(1, 4):
        for c in range(2):
            scatter_round(c, pace)
    for pace in range(4):
        for c in range(2):
            gather_round(c, pace)
    gather_end(0)

    def masked(r):
        return combined[r * n2 : (r + 1) * n2].reshape(plane, n4) * mask23[...]

    def restore(r, flat):
        hi, lo = split(flat)
        flat = dot(hi, back4[...]) + dot(lo, back4[...])
        hi, lo = split(flat)
        flat = dot(back23[...], hi) + dot(back23[...], lo)
        out[0, r] = flat.reshape(n2, n3, n4)

    restore(0, masked(0))
    gather_end(1)
    for copy in shifted:
        copy.wait_recv()
    evolved[4] = masked(4).reshape(n2, n3, n4)
    evolved[2] = (kept_row[2] * masked(2) + 0.5 * (masked(0) + evolved_row(4))).reshape(n2, n3, n4)
    restore(2, evolved_row(2))
    restore(1, kept_row[1] * masked(1) + 0.5 * (masked(0) + evolved_row(2)))
    restore(3, kept_row[3] * masked(3) + 0.5 * (evolved_row(2) + evolved_row(4)))

    started = (high, low, ring, ends, pairs, first, gpairs, gring)
    for copy in (*(copy for group in started for copy in group.values()), *shifted):
        copy.wait_send()


def shards(fields, cutoffs, weights, diffusion, courant):
    n2, n3, n4 = fields.shape[2:]
    plane = n2 * n3
    part = n2 // RING
    row = (n2, n3, n4)
    dma = pltpu.SemaphoreType.DMA
    return pl.pallas_call(
        functools.partial(kernel, row),
        out_shape=jax.ShapeDtypeStruct(fields.shape, F32),
        in_specs=[pl.BlockSpec(memory_space=pltpu.SMEM)] * 4 + [pl.BlockSpec(memory_space=pl.ANY)],
        out_specs=pl.BlockSpec(memory_space=pltpu.VMEM),
        scratch_shapes=[
            pltpu.VMEM((WINDOW, *row), F32),
            pltpu.VMEM((ROWS + 1, n2 + 2, n3, n4), F32),
            pltpu.VMEM((ROWS + 1, n2 + 2, n3, n4), F32),
            pltpu.VMEM((plane, n4), F32),
            pltpu.VMEM((ROWS + 1, *row), F32),
            pltpu.VMEM((ROWS * n2, n3, n4), F32),
            pltpu.VMEM((2, 2, 5, part, n3, n4), F32),
            pltpu.VMEM((2, 2, 2, 2, 1, n3, n4), F32),
            pltpu.VMEM((2, 2, 1, n3, n4), F32),
            pltpu.VMEM(((ROWS + 1) * n2, n3, n4), F32),
            pltpu.VMEM((n4, n4), BF16),
            pltpu.VMEM((n4, n4), BF16),
            pltpu.VMEM((n4, n4), BF16),
            pltpu.VMEM((plane, plane), BF16),
            pltpu.VMEM((n4, n4), BF16),
            pltpu.VMEM((plane, plane), BF16),
            pltpu.VMEM((plane, n4), F32),
            dma, dma((LOW,)), dma((LOW,)), dma((HIGH,)), dma((HIGH,)),
            dma((2, 2, 5)), dma((2, 2, 5)), dma((2, 2, 2, 2)), dma((2, 2, 2, 2)), dma((2, 2)), dma((2, 2)),
            dma((2, 2, 2, 2)), dma((2, 2, 2, 2)), dma((2, 2)), dma((2, 2)), dma((2, 2, 5)), dma((2, 2, 5)),
            dma((8,)), dma((8,)),
        ],
        compiler_params=pltpu.CompilerParams(
            collective_id=0, has_side_effects=True, vmem_limit_bytes=52 * 1024 * 1024
        ),
        name="advect_combine",
    )(cutoffs, weights, diffusion, courant, fields)


def solution(mesh):
    in_specs = (P("grid", "dom", None, None, None), P("grid", None), P("grid"), P(), P())
    out_specs = P("grid", "dom", None, None, None)
    return jax.shard_map(shards, mesh=mesh, in_specs=in_specs, out_specs=out_specs, check_vma=False)
```

```python
import functools
import math

import jax
import jax.numpy as jnp
from jax import lax
from jax.experimental import pallas as pl
from jax.experimental.pallas import tpu as pltpu
from jax.sharding import PartitionSpec as P

SERIES = (1.0, 2.0, 2.0, 4.0 / 3.0, 7.0 / 12.0, 1.0 / 6.0, 1.0 / 36.0)
DEGREE = 6
ROWS = 4
LOW = 6
HIGH = 7
WINDOW = LOW + ROWS + HIGH
RING = 8
SIGNS = (1.0, -1.0)
MESH = pl.DeviceIdType.MESH
F32 = jnp.float32
BF16 = jnp.bfloat16


def split(x):
    hi = x.astype(BF16)
    return hi, (x - hi.astype(F32)).astype(BF16)


def dot(a, b):
    return jnp.dot(a, b, preferred_element_type=F32)


def fine_surplus(to, source, n):
    ahead = (source - to) & (n - 1)
    near = (ahead == 1) | (ahead == n - 1)
    far = (ahead == 2) | (ahead == n - 2)
    half = ((to & 1) == 1) & near | ((to & 3) == 2) & far
    return jnp.where(ahead == 0, 1.0, jnp.where(half, -0.5, 0.0)).astype(F32)


def fine_restore(to, source, n):
    ahead = (source - to) & (n - 1)
    place = to & 3
    toward = jnp.where(place == 1, ahead, (n - ahead) & (n - 1))
    odd = jnp.where(
        toward == n - 1, 0.75, jnp.where(toward == 1, 0.5, jnp.where(toward == 3, 0.25, 0.0))
    )
    even = jnp.where((place == 2) & ((ahead == 2) | (ahead == n - 2)), 0.5, 0.0)
    return jnp.where(ahead == 0, 1.0, jnp.where((to & 1) == 1, odd, even)).astype(F32)


def coefficients(alpha, beta):
    up, down = [1.0], [1.0]
    for _ in range(DEGREE):
        up.append(up[-1] * alpha)
        down.append(down[-1] * beta)
    q = {}
    for m in range(DEGREE + 1):
        for j in range(m - DEGREE, DEGREE - m + 1):
            total = 0.0
            for l in range(abs(j), DEGREE - m + 1, 2):
                i = (l + j) // 2
                factor = SERIES[m + l] * math.comb(m + l, m) * math.comb(l, i)
                total = total + factor * up[i] * down[l - i]
            q[m, j] = total
    return q


def kernel(
    sizes,
    cutoffs, weights, diffusion, courant, fields, out,
    raw, window, held_a, held_b, product, evolved, surplus, arrived, last, paired, combined, next_row, restored,
    t_hi, t_lo, fine4, fine23, back4, back23, mask23,
    own_sem, low_send, low_recv, high_send, high_recv,
    ring_send, ring_recv, last_send, last_recv, pair_send, pair_recv,
    first_send, first_recv, gpair_send, gpair_recv, gring_send, gring_recv, row_send, row_recv,
):
    n2, n3, n4 = sizes
    half = n2 // 2
    plane = half * n3
    split_shape = (half, 2, n3 // 2, n4)
    grid_at, dom_at = lax.axis_index("grid"), lax.axis_index("dom")
    doms = lax.axis_size("dom")
    above, below = lax.rem(dom_at + 1, doms), lax.rem(dom_at + doms - 1, doms)
    z = lax.rem(grid_at, RING)
    base = grid_at - z
    other = lax.rem(base + RING, 2 * RING)
    z_next = (lax.rem(z + 1, RING), lax.rem(z + RING - 1, RING))
    beside = [((base + at, dom_at), (other + at, dom_at)) for at in z_next]
    partner = (other + z, dom_at)
    y = base // RING
    y_other = 1 - y

    barrier = pltpu.get_barrier_semaphore()
    for device in ((grid_at, above), (grid_at, below), *beside[0], *beside[1], partner):
        pl.semaphore_signal(barrier, inc=1, device_id=device, device_id_type=MESH)
    own = pltpu.make_async_copy(fields.at[0], raw, own_sem)
    own.start()
    own.wait()
    for r in range(ROWS):
        for c, sign in enumerate(SIGNS):
            window[c, LOW + r] = raw[r, :half] + sign * raw[r, half:]
    pl.semaphore_wait(barrier, 7)

    def send(source, target, device, send_sem, recv_sem):
        copy = pltpu.make_async_remote_copy(
            src_ref=source, dst_ref=target, send_sem=send_sem, recv_sem=recv_sem,
            device_id=device, device_id_type=MESH,
        )
        copy.start()
        return copy

    high, low = {}, {}

    def send_high(c, d, source):
        high[c, d] = send(
            window.at[c, source], window.at[c, LOW + ROWS + d], (grid_at, below), high_send.at[c, d], high_recv.at[c, d]
        )

    def send_low(c, d, source):
        low[c, d] = send(
            window.at[c, source], window.at[c, LOW - 1 - d], (grid_at, above), low_send.at[c, d], low_recv.at[c, d]
        )

    def send_own(c):
        for d in range(ROWS):
            send_high(c, d, LOW + d)
            send_low(c, d, LOW + ROWS - 1 - d)

    def wait_high(c, d):
        high[c, d].wait_recv()
        if d < HIGH - ROWS:
            send_high(c, ROWS + d, LOW + ROWS + d)

    def wait_low(c, d):
        low[c, d].wait_recv()
        if d < LOW - ROWS:
            send_low(c, ROWS + d, LOW - 1 - d)

    send_own(0)

    alpha = [diffusion[d] - courant[d] for d in range(4)]
    beta = [diffusion[d] + courant[d] for d in range(4)]
    centre = -2.0 * (diffusion[0] + diffusion[1] + diffusion[2] + diffusion[3])
    q = coefficients(alpha[0], beta[0])

    source4 = lax.broadcasted_iota(jnp.int32, (n4, n4), 0)
    to4 = lax.broadcasted_iota(jnp.int32, (n4, n4), 1)
    ahead4 = (source4 - to4) & (n4 - 1)
    t = jnp.where(
        ahead4 == 0, centre, jnp.where(ahead4 == 1, alpha[3], jnp.where(ahead4 == n4 - 1, beta[3], 0.0))
    )
    hi, lo = split(t)
    t_hi[...] = hi
    t_lo[...] = lo
    fine4[...] = fine_surplus(to4, source4, n4).astype(BF16)
    back4[...] = fine_restore(to4, source4, n4).astype(BF16)
    to = lax.broadcasted_iota(jnp.int32, (plane, plane), 0)
    source = lax.broadcasted_iota(jnp.int32, (plane, plane), 1)
    shift = n3.bit_length() - 1
    to2, to3, source2, source3 = to >> shift, to & (n3 - 1), source >> shift, source & (n3 - 1)
    fine = fine_surplus(to2, source2, half) * fine_surplus(to3, source3, n3)
    back = fine_restore(to2, source2, half) * fine_restore(to3, source3, n3)
    wraps = (source2 == 0) & (to2 > half // 2)
    for c, sign in enumerate(SIGNS):
        fine23[c] = jnp.where(wraps, sign * fine, fine).astype(BF16)
        back23[c] = jnp.where(wraps, sign * back, back).astype(BF16)
    line = lax.broadcasted_iota(jnp.int32, (plane, n4), 0)
    cell = lax.broadcasted_iota(jnp.int32, (plane, n4), 1)
    stride = [jnp.left_shift(jnp.int32(1), cutoffs[0, d]) for d in range(4)]
    off = ((line >> shift) & (stride[1] - 1)) | (line & (n3 - 1) & (stride[2] - 1)) | (cell & (stride[3] - 1))
    mask23[...] = jnp.where(off == 0, 1.0, 0.0).astype(F32)
    kept_row = [jnp.where((r & (stride[0] - 1)) == 0, 1.0, 0.0).astype(F32) for r in range(ROWS)]
    weight = weights[0].astype(F32) * (0.5 / (2 * RING))

    block = 4

    def level(c, d, first_row, stride_row, count):
        m = DEGREE - d
        now, then = (held_a, held_b) if d % 2 == 0 else (held_b, held_a)

        def row(index, carry):
            r = first_row + index * stride_row
            if d > 0:
                hi, lo = split(now[r, 1 : half + 1].reshape(plane, n4))
                product[...] = dot(hi, t_hi[...]) + dot(lo, t_hi[...]) + dot(hi, t_lo[...])
            for i in range(0, half, block):
                total = None
                for j in range(-d, d + 1):
                    term = q[m, j] * window[c, LOW + r + j, i : i + block]
                    total = term if total is None else total + term
                if d > 0:
                    here = now[r, i + 1 : i + 1 + block]
                    total = total + product[i * n3 : (i + block) * n3].reshape(block, n3, n4)
                    total = total + alpha[1] * now[r, i + 2 : i + 2 + block] + beta[1] * now[r, i : i + block]
                    total = total + alpha[2] * pltpu.roll(here, n3 - 1, 1) + beta[2] * pltpu.roll(here, 1, 1)
                if m > 0:
                    then[r, i + 1 : i + 1 + block] = total
                else:
                    evolved[r, i : i + block] = total
            if m > 0:
                then[r, 0] = SIGNS[c] * then[r, half]
                then[r, half + 1] = SIGNS[c] * then[r, 1]
            return carry

        if count == 1:
            row(0, 0)
        else:
            lax.fori_loop(0, count, row, 0)

    def evolve_start(c):
        level(c, 0, 1, 1, 2)

    def evolve_step(c, d):
        level(c, d, 0, 3, 2)
        level(c, d + 1, 1, 1, 2)
        if d > 0:
            level(c, d - 1, 4, 1, 1)
        wait_high(c, d)
        wait_low(c, d)

    def evolve_end(c):
        level(c, DEGREE, 0, 3, 2)
        level(c, DEGREE - 1, 4, 1, 1)
        surplus_of(c, 0, evolved_row(0))
        surplus_of(c, 1, evolved_row(1) - 0.5 * (evolved_row(0) + evolved_row(2)))
        wait_high(c, DEGREE)
        level(c, DEGREE, 4, 1, 1)
        surplus_of(c, 2, evolved_row(2) - 0.5 * (evolved_row(0) + evolved_row(4)))
        surplus_of(c, 3, evolved_row(3) - 0.5 * (evolved_row(2) + evolved_row(4)))

    def surplus_of(c, r, flat):
        hi, lo = split(flat)
        flat = dot(hi, fine4[...]) + dot(lo, fine4[...])
        hi, lo = split(flat)
        flat = dot(fine23[c], hi) + dot(fine23[c], lo)
        flat = flat * (mask23[...] * (weight * kept_row[r]))
        surplus[c, r % 2, :, :, r // 2] = flat.reshape(split_shape)

    def evolved_row(r):
        return evolved[r].reshape(plane, n4)

    def at_z(offset):
        return lax.rem(z + offset + RING, RING)

    order = [[(0, 4), (1, 3), (0, 3), (1, 2), (0, 2), (1, 1), (0, 1)]]
    order.append([(1 - h, -o) for h, o in order[0]])
    gorder = [[(0, 0), (1, 0), (0, -1), (1, -1), (0, -2), (1, -2), (0, -3)]]
    gorder.append([(1 - h, -o) for h, o in gorder[0]])
    steps, inner = len(order[0]), len(order[0]) - 2
    ring, ends, pairs, first, gpairs, gring, shifted = {}, {}, {}, {}, {}, {}, ({}, {})

    def scatter_round(c, pace):
        for step in range(2 * pace, min(2 * pace + 2, steps)):
            for way in range(2):
                h, offset = order[way][step]
                where = at_z(offset)
                if step >= 2:
                    ring[c, way, step - 2].wait_recv()
                    surplus[c, h, where] = surplus[c, h, where] + arrived[c, way, step - 2]
                if step < inner:
                    ring[c, way, step] = send(
                        surplus.at[c, h, where], arrived.at[c, way, step], beside[way][0],
                        ring_send.at[c, way, step], ring_recv.at[c, way, step],
                    )
                    continue
                for across, part in ((1, y_other), (0, y)):
                    ends[c, way, h, across] = send(
                        surplus.at[c, h, where, part], last.at[c, way, h, across], beside[way][across],
                        last_send.at[c, way, h, across], last_recv.at[c, way, h, across],
                    )
        if pace == 0:
            for h in range(2):
                pairs[c, h] = send(
                    surplus.at[c, h, z, y_other], paired.at[c, h], partner, pair_send.at[c, h], pair_recv.at[c, h]
                )

    def finish(c, h):
        pairs[c, h].wait_recv()
        total = surplus[c, h, z, y] + paired[c, h]
        for across in range(2):
            for way in range(2):
                ends[c, way, h, across].wait_recv()
            total = total + (last[c, 0, h, across] + last[c, 1, h, across])
        combined[c, h, z, y] = total

    def shift_row(c, offset):
        index = len(shifted[c])
        where = at_z(offset)
        shifted[c][index] = send(
            combined.at[c, 0, where, :, 0], next_row.at[c, where], (grid_at, below),
            row_send.at[c, index], row_recv.at[c, index],
        )

    def landed(c, way, step):
        h, offset = gorder[way][step]
        if step < 2:
            for across in range(2):
                first[c, way, h, across].wait_recv()
        else:
            gring[c, way, step - 2].wait_recv()
        if h == 0:
            shift_row(c, offset - (1 - 2 * way))

    def gather_round(c, pace):
        if pace == 0:
            for h in range(2):
                finish(c, h)
                mine = combined.at[c, h, z, y]
                for across in (1, 0):
                    for way in range(2):
                        first[c, way, h, across] = send(
                            mine, mine, beside[way][across],
                            first_send.at[c, way, h, across], first_recv.at[c, way, h, across],
                        )
                gpairs[c, h] = send(mine, mine, partner, gpair_send.at[c, h], gpair_recv.at[c, h])
            return
        for step in range(2 * pace, min(2 * pace + 2, steps)):
            for way in range(2):
                landed(c, way, step - 2)
                h, offset = gorder[way][step]
                where = combined.at[c, h, at_z(offset)]
                gring[c, way, step - 2] = send(
                    where, where, beside[way][0], gring_send.at[c, way, step - 2], gring_recv.at[c, way, step - 2]
                )
        if pace == 1:
            for h in range(2):
                gpairs[c, h].wait_recv()
            shift_row(c, 0)

    def gather_end(c):
        for step in (inner, inner + 1):
            for way in range(2):
                landed(c, way, step)

    def masked(c, r):
        if r == ROWS:
            return next_row[c].reshape(plane, n4) * mask23[...]
        return combined[c, r % 2, :, :, r // 2].reshape(plane, n4) * mask23[...]

    def restore(c, r, flat):
        hi, lo = split(flat)
        flat = dot(hi, back4[...]) + dot(lo, back4[...])
        hi, lo = split(flat)
        flat = (dot(back23[c], hi) + dot(back23[c], lo)).reshape(half, n3, n4)
        if c == 0:
            restored[r] = flat
        else:
            out[0, r, :half] = restored[r] + flat
            out[0, r, half:] = restored[r] - flat

    def restore_unit(c):
        restore(c, 0, masked(c, 0))
        for copy in shifted[c].values():
            copy.wait_recv()
        evolved[4] = masked(c, 4).reshape(half, n3, n4)
        evolved[2] = (kept_row[2] * masked(c, 2) + 0.5 * (masked(c, 0) + evolved_row(4))).reshape(half, n3, n4)
        restore(c, 2, evolved_row(2))
        restore(c, 1, kept_row[1] * masked(c, 1) + 0.5 * (masked(c, 0) + evolved_row(2)))
        restore(c, 3, kept_row[3] * masked(c, 3) + 0.5 * (evolved_row(2) + evolved_row(4)))

    evolve_start(0)
    for d in range(DEGREE):
        evolve_step(0, d)
        if d == 2:
            send_own(1)
    evolve_end(0)
    scatter_round(0, 0)
    evolve_start(1)
    for d in range(DEGREE):
        evolve_step(1, d)
        if d == 2:
            scatter_round(0, 1)
        if d == 4:
            scatter_round(0, 2)
    evolve_end(1)
    scatter_round(1, 0)
    scatter_round(0, 3)
    scatter_round(1, 1)
    gather_round(0, 0)
    scatter_round(1, 2)
    gather_round(0, 1)
    scatter_round(1, 3)
    gather_round(0, 2)
    gather_round(1, 0)
    gather_round(0, 3)
    gather_round(1, 1)
    gather_end(0)
    restore_unit(0)
    gather_round(1, 2)
    gather_round(1, 3)
    gather_end(1)
    restore_unit(1)

    started = (high, low, ring, ends, pairs, first, gpairs, gring, *shifted)
    for copy in (copy for group in started for copy in group.values()):
        copy.wait_send()


def shards(fields, cutoffs, weights, diffusion, courant):
    n2, n3, n4 = fields.shape[2:]
    half = n2 // 2
    plane = half * n3
    row = (half, n3, n4)
    tile = (2, n3 // 2, n4)
    dma = pltpu.SemaphoreType.DMA
    return pl.pallas_call(
        functools.partial(kernel, (n2, n3, n4)),
        out_shape=jax.ShapeDtypeStruct(fields.shape, F32),
        in_specs=[pl.BlockSpec(memory_space=pltpu.SMEM)] * 4 + [pl.BlockSpec(memory_space=pl.ANY)],
        out_specs=pl.BlockSpec(memory_space=pltpu.VMEM),
        scratch_shapes=[
            pltpu.VMEM((ROWS, n2, n3, n4), F32),
            pltpu.VMEM((2, WINDOW, *row), F32),
            pltpu.VMEM((ROWS + 1, half + 2, n3, n4), F32),
            pltpu.VMEM((ROWS + 1, half + 2, n3, n4), F32),
            pltpu.VMEM((plane, n4), F32),
            pltpu.VMEM((ROWS + 1, *row), F32),
            pltpu.VMEM((2, 2, half, 2, *tile), F32),
            pltpu.VMEM((2, 2, 5, 2, *tile), F32),
            pltpu.VMEM((2, 2, 2, 2, *tile), F32),
            pltpu.VMEM((2, 2, *tile), F32),
            pltpu.VMEM((2, 2, half, 2, *tile), F32),
            pltpu.VMEM((2, half, *tile), F32),
            pltpu.VMEM((ROWS, *row), F32),
            pltpu.VMEM((n4, n4), BF16),
            pltpu.VMEM((n4, n4), BF16),
            pltpu.VMEM((n4, n4), BF16),
            pltpu.VMEM((2, plane, plane), BF16),
            pltpu.VMEM((n4, n4), BF16),
            pltpu.VMEM((2, plane, plane), BF16),
            pltpu.VMEM((plane, n4), F32),
            dma, dma((2, LOW)), dma((2, LOW)), dma((2, HIGH)), dma((2, HIGH)),
            dma((2, 2, 5)), dma((2, 2, 5)), dma((2, 2, 2, 2)), dma((2, 2, 2, 2)), dma((2, 2)), dma((2, 2)),
            dma((2, 2, 2, 2)), dma((2, 2, 2, 2)), dma((2, 2)), dma((2, 2)), dma((2, 2, 5)), dma((2, 2, 5)),
            dma((2, 8)), dma((2, 8)),
        ],
        compiler_params=pltpu.CompilerParams(
            collective_id=0, has_side_effects=True, vmem_limit_bytes=52 * 1024 * 1024
        ),
        name="advect_combine",
    )(cutoffs, weights, diffusion, courant, fields)


def solution(mesh):
    in_specs = (P("grid", "dom", None, None, None), P("grid", None), P("grid"), P(), P())
    out_specs = P("grid", "dom", None, None, None)
    return jax.shard_map(shards, mesh=mesh, in_specs=in_specs, out_specs=out_specs, check_vma=False)
```

```python
import functools
import math

import jax
import jax.numpy as jnp
from jax import lax
from jax.experimental import pallas as pl
from jax.experimental.pallas import tpu as pltpu
from jax.sharding import PartitionSpec as P

SERIES = (1.0, 2.0, 2.0, 4.0 / 3.0, 7.0 / 12.0, 1.0 / 6.0, 1.0 / 36.0)
DEGREE = 6
ROWS = 4
LOW = 6
HIGH = 7
WINDOW = LOW + ROWS + HIGH
RING = 8
MESH = pl.DeviceIdType.MESH
F32 = jnp.float32
BF16 = jnp.bfloat16


def split(x):
    hi = x.astype(BF16)
    return hi, (x - hi.astype(F32)).astype(BF16)


def dot(a, b):
    return jnp.dot(a, b, preferred_element_type=F32)


def fine_surplus(to, source, n):
    ahead = (source - to) & (n - 1)
    near = (ahead == 1) | (ahead == n - 1)
    far = (ahead == 2) | (ahead == n - 2)
    half = ((to & 1) == 1) & near | ((to & 3) == 2) & far
    return jnp.where(ahead == 0, 1.0, jnp.where(half, -0.5, 0.0)).astype(F32)


def fine_restore(to, source, n):
    ahead = (source - to) & (n - 1)
    place = to & 3
    toward = jnp.where(place == 1, ahead, (n - ahead) & (n - 1))
    odd = jnp.where(
        toward == n - 1, 0.75, jnp.where(toward == 1, 0.5, jnp.where(toward == 3, 0.25, 0.0))
    )
    even = jnp.where((place == 2) & ((ahead == 2) | (ahead == n - 2)), 0.5, 0.0)
    return jnp.where(ahead == 0, 1.0, jnp.where((to & 1) == 1, odd, even)).astype(F32)


def coefficients(alpha, beta):
    up, down = [1.0], [1.0]
    for _ in range(DEGREE):
        up.append(up[-1] * alpha)
        down.append(down[-1] * beta)
    q = {}
    for m in range(DEGREE + 1):
        for j in range(m - DEGREE, DEGREE - m + 1):
            total = 0.0
            for l in range(abs(j), DEGREE - m + 1, 2):
                i = (l + j) // 2
                factor = SERIES[m + l] * math.comb(m + l, m) * math.comb(l, i)
                total = total + factor * up[i] * down[l - i]
            q[m, j] = total
    return q


def kernel(
    sizes,
    cutoffs, weights, diffusion, courant, fields, out,
    window, held_a, held_b, product, evolved, surplus, arrived, last, paired, combined,
    t_hi, t_lo, fine4, fine23, back4, back23, mask23,
    own_sem, low_send, low_recv, high_send, high_recv,
    ring_send, ring_recv, last_send, last_recv, pair_send, pair_recv,
    first_send, first_recv, gpair_send, gpair_recv, gring_send, gring_recv, row_send, row_recv,
):
    n2, n3, n4 = sizes
    plane = n2 * n3
    part = n2 // RING
    grid_at, dom_at = lax.axis_index("grid"), lax.axis_index("dom")
    doms = lax.axis_size("dom")
    above, below = lax.rem(dom_at + 1, doms), lax.rem(dom_at + doms - 1, doms)
    z = lax.rem(grid_at, RING)
    base = grid_at - z
    other = lax.rem(base + RING, 2 * RING)
    z_next = (lax.rem(z + 1, RING), lax.rem(z + RING - 1, RING))
    beside = [((base + at, dom_at), (other + at, dom_at)) for at in z_next]
    partner = (other + z, dom_at)
    y = base // RING
    y_other = 1 - y

    barrier = pltpu.get_barrier_semaphore()
    for device in ((grid_at, above), (grid_at, below), *beside[0], *beside[1], partner):
        pl.semaphore_signal(barrier, inc=1, device_id=device, device_id_type=MESH)
    own = pltpu.make_async_copy(fields.at[0], window.at[LOW : LOW + ROWS], own_sem)
    own.start()
    pl.semaphore_wait(barrier, 7)

    def send(source, target, device, send_sem, recv_sem):
        copy = pltpu.make_async_remote_copy(
            src_ref=source, dst_ref=target, send_sem=send_sem, recv_sem=recv_sem,
            device_id=device, device_id_type=MESH,
        )
        copy.start()
        return copy

    high, low = {}, {}
    for d in range(ROWS):
        high[d] = send(
            fields.at[0, d], window.at[LOW + ROWS + d], (grid_at, below), high_send.at[d], high_recv.at[d]
        )
        low[d] = send(
            fields.at[0, ROWS - 1 - d], window.at[LOW - 1 - d], (grid_at, above), low_send.at[d], low_recv.at[d]
        )
    alpha = [diffusion[d] - courant[d] for d in range(4)]
    beta = [diffusion[d] + courant[d] for d in range(4)]
    centre = -2.0 * (diffusion[0] + diffusion[1] + diffusion[2] + diffusion[3])
    q = coefficients(alpha[0], beta[0])

    source4 = lax.broadcasted_iota(jnp.int32, (n4, n4), 0)
    to4 = lax.broadcasted_iota(jnp.int32, (n4, n4), 1)
    ahead4 = (source4 - to4) & (n4 - 1)
    t = jnp.where(
        ahead4 == 0, centre, jnp.where(ahead4 == 1, alpha[3], jnp.where(ahead4 == n4 - 1, beta[3], 0.0))
    )
    hi, lo = split(t)
    t_hi[...] = hi
    t_lo[...] = lo
    fine4[...] = fine_surplus(to4, source4, n4).astype(BF16)
    back4[...] = fine_restore(to4, source4, n4).astype(BF16)
    to = lax.broadcasted_iota(jnp.int32, (plane, plane), 0)
    source = lax.broadcasted_iota(jnp.int32, (plane, plane), 1)
    shift = n3.bit_length() - 1
    to2, to3, source2, source3 = to >> shift, to & (n3 - 1), source >> shift, source & (n3 - 1)
    fine23[...] = (fine_surplus(to2, source2, n2) * fine_surplus(to3, source3, n3)).astype(BF16)
    back23[...] = (fine_restore(to2, source2, n2) * fine_restore(to3, source3, n3)).astype(BF16)
    line = lax.broadcasted_iota(jnp.int32, (plane, n4), 0)
    cell = lax.broadcasted_iota(jnp.int32, (plane, n4), 1)
    stride = [jnp.left_shift(jnp.int32(1), cutoffs[0, d]) for d in range(4)]
    off = ((line >> shift) & (stride[1] - 1)) | (line & (n3 - 1) & (stride[2] - 1)) | (cell & (stride[3] - 1))
    mask23[...] = jnp.where(off == 0, 1.0, 0.0).astype(F32)
    kept_row = [jnp.where((r & (stride[0] - 1)) == 0, 1.0, 0.0).astype(F32) for r in range(ROWS)]
    weight = weights[0].astype(F32) * (1.0 / (2 * RING))

    own.wait()
    block = 4

    def wait_high(d):
        high[d].wait_recv()
        if d < HIGH - ROWS:
            high[ROWS + d] = send(
                window.at[LOW + ROWS + d], window.at[LOW + 2 * ROWS + d], (grid_at, below),
                high_send.at[ROWS + d], high_recv.at[ROWS + d],
            )

    def wait_low(d):
        low[d].wait_recv()
        if d < LOW - ROWS:
            low[ROWS + d] = send(
                window.at[LOW - 1 - d], window.at[LOW - 1 - ROWS - d], (grid_at, above),
                low_send.at[ROWS + d], low_recv.at[ROWS + d],
            )

    def level(d, first, stride, count, missing=None):
        m = DEGREE - d
        now, then = (held_a, held_b) if d % 2 == 0 else (held_b, held_a)

        def row(index, carry):
            r = first + index * stride
            if d > 0:
                hi, lo = split(now[r, 1 : n2 + 1].reshape(plane, n4))
                product[...] = dot(hi, t_hi[...]) + dot(lo, t_hi[...]) + dot(hi, t_lo[...])
            for i in range(0, n2, block):
                total = None
                for j in range(-d, d + 1):
                    if j == missing:
                        continue
                    term = q[m, j] * window[LOW + r + j, i : i + block]
                    total = term if total is None else total + term
                if d > 0:
                    here = now[r, i + 1 : i + 1 + block]
                    total = total + product[i * n3 : (i + block) * n3].reshape(block, n3, n4)
                    total = total + alpha[1] * now[r, i + 2 : i + 2 + block] + beta[1] * now[r, i : i + block]
                    total = total + alpha[2] * pltpu.roll(here, n3 - 1, 1) + beta[2] * pltpu.roll(here, 1, 1)
                if m > 0:
                    then[r, i + 1 : i + 1 + block] = total
                else:
                    evolved[r, i : i + block] = total
            if m > 0:
                then[r, 0] = then[r, n2]
                then[r, n2 + 1] = then[r, 1]
            return carry

        if count == 1:
            row(0, 0)
        else:
            lax.fori_loop(0, count, row, 0)

    level(0, 1, 1, 2)
    for d in range(DEGREE - 1):
        level(d, 0, 3, 2)
        level(d + 1, 1, 1, 2)
        if d > 0:
            level(d - 1, 4, 1, 1)
        wait_high(d)
        wait_low(d)
    level(DEGREE - 1, 0, 3, 2)
    level(DEGREE, 1, 1, 2)
    level(DEGREE - 2, 4, 1, 1)

    level(DEGREE, 0, 1, 1, -DEGREE)
    level(DEGREE, 3, 1, 1, DEGREE)

    def farthest(r, j):
        evolved[r] = evolved[r] + q[0, j] * window[LOW + r + j]

    def surplus_of(r, flat):
        hi, lo = split(flat)
        flat = dot(hi, fine4[...]) + dot(lo, fine4[...])
        hi, lo = split(flat)
        flat = dot(fine23[...], hi) + dot(fine23[...], lo)
        flat = flat * (mask23[...] * (weight * kept_row[r]))
        surplus[r * n2 : (r + 1) * n2] = flat.reshape(n2, n3, n4)

    def evolved_row(r):
        return evolved[r].reshape(plane, n4)

    def piece(c, h, offset):
        return pl.ds((2 * c + h) * n2 + lax.rem(z + offset + RING, RING) * part, part)

    def layer(c, h, offset, at):
        return pl.ds((2 * c + h) * n2 + lax.rem(z + offset + RING, RING) * part + at, 1)

    order = [[(0, 4), (1, 3), (0, 3), (1, 2), (0, 2), (1, 1), (0, 1)]]
    order.append([(1 - h, -o) for h, o in order[0]])
    gorder = [[(0, 0), (1, 0), (0, -1), (1, -1), (0, -2), (1, -2), (0, -3)]]
    gorder.append([(1 - h, -o) for h, o in gorder[0]])
    steps, inner = len(order[0]), len(order[0]) - 2
    ring, ends, pairs, first, gpairs, gring, shifted = {}, {}, {}, {}, {}, {}, []

    def scatter_round(c, pace):
        for step in range(2 * pace, min(2 * pace + 2, steps)):
            for way in range(2):
                h, offset = order[way][step]
                where = piece(c, h, offset)
                if step >= 2:
                    ring[c, way, step - 2].wait_recv()
                    surplus[where] = surplus[where] + arrived[c, way, step - 2]
                if step < inner:
                    ring[c, way, step] = send(
                        surplus.at[where], arrived.at[c, way, step], beside[way][0],
                        ring_send.at[c, way, step], ring_recv.at[c, way, step],
                    )
                    continue
                for across, at in ((1, y_other), (0, y)):
                    ends[c, way, h, across] = send(
                        surplus.at[layer(c, h, offset, at)], last.at[c, way, h, across], beside[way][across],
                        last_send.at[c, way, h, across], last_recv.at[c, way, h, across],
                    )
        if pace == 0:
            for h in range(2):
                pairs[c, h] = send(
                    surplus.at[layer(c, h, 0, y_other)], paired.at[c, h], partner,
                    pair_send.at[c, h], pair_recv.at[c, h],
                )

    def finish(c, h):
        pairs[c, h].wait_recv()
        mine = layer(c, h, 0, y)
        total = surplus[mine] + paired[c, h]
        for across in range(2):
            for way in range(2):
                ends[c, way, h, across].wait_recv()
            total = total + (last[c, 0, h, across] + last[c, 1, h, across])
        combined[mine] = total

    def shift_row(offset):
        index = len(shifted)
        where = piece(0, 0, offset)
        target = pl.ds(ROWS * n2 + lax.rem(z + offset + RING, RING) * part, part)
        shifted.append(
            send(combined.at[where], combined.at[target], (grid_at, below), row_send.at[index], row_recv.at[index])
        )

    def landed(c, way, step):
        h, offset = gorder[way][step]
        if step < 2:
            for across in range(2):
                first[c, way, h, across].wait_recv()
        else:
            gring[c, way, step - 2].wait_recv()
        if c == 0 and h == 0:
            shift_row(offset - (1 - 2 * way))

    def gather_round(c, pace):
        if pace == 0:
            for h in range(2):
                finish(c, h)
                mine = combined.at[layer(c, h, 0, y)]
                for across in (1, 0):
                    for way in range(2):
                        first[c, way, h, across] = send(
                            mine, mine, beside[way][across],
                            first_send.at[c, way, h, across], first_recv.at[c, way, h, across],
                        )
                gpairs[c, h] = send(mine, mine, partner, gpair_send.at[c, h], gpair_recv.at[c, h])
            return
        for step in range(2 * pace, min(2 * pace + 2, steps)):
            for way in range(2):
                landed(c, way, step - 2)
                where = combined.at[piece(c, *gorder[way][step])]
                gring[c, way, step - 2] = send(
                    where, where, beside[way][0], gring_send.at[c, way, step - 2], gring_recv.at[c, way, step - 2]
                )
        if pace == 1:
            for h in range(2):
                gpairs[c, h].wait_recv()
            if c == 0:
                shift_row(0)

    def gather_end(c):
        for step in (inner, inner + 1):
            for way in range(2):
                landed(c, way, step)

    wait_low(DEGREE - 1)
    farthest(0, -DEGREE)
    surplus_of(0, evolved_row(0))
    surplus_of(1, evolved_row(1) - 0.5 * (evolved_row(0) + evolved_row(2)))
    scatter_round(0, 0)
    wait_high(DEGREE - 1)
    farthest(3, DEGREE)
    level(DEGREE - 1, 4, 1, 1)
    level(DEGREE, 4, 1, 1, DEGREE)
    wait_high(DEGREE)
    farthest(4, DEGREE)
    surplus_of(2, evolved_row(2) - 0.5 * (evolved_row(0) + evolved_row(4)))
    surplus_of(3, evolved_row(3) - 0.5 * (evolved_row(2) + evolved_row(4)))
    scatter_round(1, 0)
    for pace in range(1, 4):
        for c in range(2):
            scatter_round(c, pace)
    for pace in range(4):
        for c in range(2):
            gather_round(c, pace)
    gather_end(0)

    def masked(r):
        return combined[r * n2 : (r + 1) * n2].reshape(plane, n4) * mask23[...]

    def restore(r, flat):
        hi, lo = split(flat)
        flat = dot(hi, back4[...]) + dot(lo, back4[...])
        hi, lo = split(flat)
        flat = dot(back23[...], hi) + dot(back23[...], lo)
        out[0, r] = flat.reshape(n2, n3, n4)

    restore(0, masked(0))
    gather_end(1)
    for copy in shifted:
        copy.wait_recv()
    evolved[4] = masked(4).reshape(n2, n3, n4)
    evolved[2] = (kept_row[2] * masked(2) + 0.5 * (masked(0) + evolved_row(4))).reshape(n2, n3, n4)
    restore(2, evolved_row(2))
    restore(1, kept_row[1] * masked(1) + 0.5 * (masked(0) + evolved_row(2)))
    restore(3, kept_row[3] * masked(3) + 0.5 * (evolved_row(2) + evolved_row(4)))

    started = (high, low, ring, ends, pairs, first, gpairs, gring)
    for copy in (*(copy for group in started for copy in group.values()), *shifted):
        copy.wait_send()


def shards(fields, cutoffs, weights, diffusion, courant):
    n2, n3, n4 = fields.shape[2:]
    plane = n2 * n3
    part = n2 // RING
    row = (n2, n3, n4)
    dma = pltpu.SemaphoreType.DMA
    return pl.pallas_call(
        functools.partial(kernel, row),
        out_shape=jax.ShapeDtypeStruct(fields.shape, F32),
        in_specs=[pl.BlockSpec(memory_space=pltpu.SMEM)] * 4 + [pl.BlockSpec(memory_space=pl.ANY)],
        out_specs=pl.BlockSpec(memory_space=pltpu.VMEM),
        scratch_shapes=[
            pltpu.VMEM((WINDOW, *row), F32),
            pltpu.VMEM((ROWS + 1, n2 + 2, n3, n4), F32),
            pltpu.VMEM((ROWS + 1, n2 + 2, n3, n4), F32),
            pltpu.VMEM((plane, n4), F32),
            pltpu.VMEM((ROWS + 1, *row), F32),
            pltpu.VMEM((ROWS * n2, n3, n4), F32),
            pltpu.VMEM((2, 2, 5, part, n3, n4), F32),
            pltpu.VMEM((2, 2, 2, 2, 1, n3, n4), F32),
            pltpu.VMEM((2, 2, 1, n3, n4), F32),
            pltpu.VMEM(((ROWS + 1) * n2, n3, n4), F32),
            pltpu.VMEM((n4, n4), BF16),
            pltpu.VMEM((n4, n4), BF16),
            pltpu.VMEM((n4, n4), BF16),
            pltpu.VMEM((plane, plane), BF16),
            pltpu.VMEM((n4, n4), BF16),
            pltpu.VMEM((plane, plane), BF16),
            pltpu.VMEM((plane, n4), F32),
            dma, dma((LOW,)), dma((LOW,)), dma((HIGH,)), dma((HIGH,)),
            dma((2, 2, 5)), dma((2, 2, 5)), dma((2, 2, 2, 2)), dma((2, 2, 2, 2)), dma((2, 2)), dma((2, 2)),
            dma((2, 2, 2, 2)), dma((2, 2, 2, 2)), dma((2, 2)), dma((2, 2)), dma((2, 2, 5)), dma((2, 2, 5)),
            dma((8,)), dma((8,)),
        ],
        compiler_params=pltpu.CompilerParams(
            collective_id=0, has_side_effects=True, vmem_limit_bytes=52 * 1024 * 1024
        ),
        name="advect_combine",
    )(cutoffs, weights, diffusion, courant, fields)


def solution(mesh):
    in_specs = (P("grid", "dom", None, None, None), P("grid", None), P("grid"), P(), P())
    out_specs = P("grid", "dom", None, None, None)
    return jax.shard_map(shards, mesh=mesh, in_specs=in_specs, out_specs=out_specs, check_vma=False)
```

```python
import functools
import math

import jax
import jax.numpy as jnp
from jax import lax
from jax.experimental import pallas as pl
from jax.experimental.pallas import tpu as pltpu
from jax.sharding import PartitionSpec as P

SERIES = (1.0, 2.0, 2.0, 4.0 / 3.0, 7.0 / 12.0, 1.0 / 6.0, 1.0 / 36.0)
DEGREE = 6
ROWS = 4
LOW = 6
HIGH = 7
WINDOW = LOW + ROWS + HIGH
RING = 8
MESH = pl.DeviceIdType.MESH
F32 = jnp.float32
BF16 = jnp.bfloat16


def split(x):
    hi = x.astype(BF16)
    return hi, (x - hi.astype(F32)).astype(BF16)


def dot(a, b):
    return jnp.dot(a, b, preferred_element_type=F32)


def fine_surplus(to, source, n):
    ahead = (source - to) & (n - 1)
    near = (ahead == 1) | (ahead == n - 1)
    far = (ahead == 2) | (ahead == n - 2)
    half = ((to & 1) == 1) & near | ((to & 3) == 2) & far
    return jnp.where(ahead == 0, 1.0, jnp.where(half, -0.5, 0.0)).astype(F32)


def fine_restore(to, source, n):
    ahead = (source - to) & (n - 1)
    place = to & 3
    toward = jnp.where(place == 1, ahead, (n - ahead) & (n - 1))
    odd = jnp.where(
        toward == n - 1, 0.75, jnp.where(toward == 1, 0.5, jnp.where(toward == 3, 0.25, 0.0))
    )
    even = jnp.where((place == 2) & ((ahead == 2) | (ahead == n - 2)), 0.5, 0.0)
    return jnp.where(ahead == 0, 1.0, jnp.where((to & 1) == 1, odd, even)).astype(F32)


def coefficients(alpha, beta):
    up, down = [1.0], [1.0]
    for _ in range(DEGREE):
        up.append(up[-1] * alpha)
        down.append(down[-1] * beta)
    q = {}
    for m in range(DEGREE + 1):
        for j in range(m - DEGREE, DEGREE - m + 1):
            total = 0.0
            for l in range(abs(j), DEGREE - m + 1, 2):
                i = (l + j) // 2
                factor = SERIES[m + l] * math.comb(m + l, m) * math.comb(l, i)
                total = total + factor * up[i] * down[l - i]
            q[m, j] = total
    return q


def kernel(
    sizes,
    cutoffs, weights, diffusion, courant, fields, out,
    window, held_a, held_b, product, evolved, surplus, arrived, last, paired, combined,
    t_hi, t_lo, fine4, fine23, back4, back23, mask23,
    own_sem, low_send, low_recv, high_send, high_recv,
    ring_send, ring_recv, last_send, last_recv, pair_send, pair_recv,
    first_send, first_recv, gpair_send, gpair_recv, gring_send, gring_recv, row_send, row_recv,
):
    n2, n3, n4 = sizes
    plane = n2 * n3
    part = n2 // RING
    grid_at, dom_at = lax.axis_index("grid"), lax.axis_index("dom")
    doms = lax.axis_size("dom")
    above, below = lax.rem(dom_at + 1, doms), lax.rem(dom_at + doms - 1, doms)
    z = lax.rem(grid_at, RING)
    base = grid_at - z
    other = lax.rem(base + RING, 2 * RING)
    z_next = (lax.rem(z + 1, RING), lax.rem(z + RING - 1, RING))
    beside = [((base + at, dom_at), (other + at, dom_at)) for at in z_next]
    two_on = [(base + lax.rem(z + hops, RING), dom_at) for hops in (2, RING - 2)]
    partner = (other + z, dom_at)
    y = base // RING
    y_other = 1 - y

    barrier = pltpu.get_barrier_semaphore()
    for device in ((grid_at, above), (grid_at, below), *beside[0], *beside[1], *two_on, partner):
        pl.semaphore_signal(barrier, inc=1, device_id=device, device_id_type=MESH)
    own = pltpu.make_async_copy(fields.at[0], window.at[LOW : LOW + ROWS], own_sem)
    own.start()
    pl.semaphore_wait(barrier, 9)

    def send(source, target, device, send_sem, recv_sem):
        copy = pltpu.make_async_remote_copy(
            src_ref=source, dst_ref=target, send_sem=send_sem, recv_sem=recv_sem,
            device_id=device, device_id_type=MESH,
        )
        copy.start()
        return copy

    high, low = {}, {}
    for d in range(ROWS):
        high[d] = send(
            fields.at[0, d], window.at[LOW + ROWS + d], (grid_at, below), high_send.at[d], high_recv.at[d]
        )
        low[d] = send(
            fields.at[0, ROWS - 1 - d], window.at[LOW - 1 - d], (grid_at, above), low_send.at[d], low_recv.at[d]
        )
    alpha = [diffusion[d] - courant[d] for d in range(4)]
    beta = [diffusion[d] + courant[d] for d in range(4)]
    centre = -2.0 * (diffusion[0] + diffusion[1] + diffusion[2] + diffusion[3])
    q = coefficients(alpha[0], beta[0])

    source4 = lax.broadcasted_iota(jnp.int32, (n4, n4), 0)
    to4 = lax.broadcasted_iota(jnp.int32, (n4, n4), 1)
    ahead4 = (source4 - to4) & (n4 - 1)
    t = jnp.where(
        ahead4 == 0, centre, jnp.where(ahead4 == 1, alpha[3], jnp.where(ahead4 == n4 - 1, beta[3], 0.0))
    )
    hi, lo = split(t)
    t_hi[...] = hi
    t_lo[...] = lo
    fine4[...] = fine_surplus(to4, source4, n4).astype(BF16)
    back4[...] = fine_restore(to4, source4, n4).astype(BF16)
    to = lax.broadcasted_iota(jnp.int32, (plane, plane), 0)
    source = lax.broadcasted_iota(jnp.int32, (plane, plane), 1)
    shift = n3.bit_length() - 1
    to2, to3, source2, source3 = to >> shift, to & (n3 - 1), source >> shift, source & (n3 - 1)
    fine23[...] = (fine_surplus(to2, source2, n2) * fine_surplus(to3, source3, n3)).astype(BF16)
    back23[...] = (fine_restore(to2, source2, n2) * fine_restore(to3, source3, n3)).astype(BF16)
    line = lax.broadcasted_iota(jnp.int32, (plane, n4), 0)
    cell = lax.broadcasted_iota(jnp.int32, (plane, n4), 1)
    stride = [jnp.left_shift(jnp.int32(1), cutoffs[0, d]) for d in range(4)]
    off = ((line >> shift) & (stride[1] - 1)) | (line & (n3 - 1) & (stride[2] - 1)) | (cell & (stride[3] - 1))
    mask23[...] = jnp.where(off == 0, 1.0, 0.0).astype(F32)
    kept_row = [jnp.where((r & (stride[0] - 1)) == 0, 1.0, 0.0).astype(F32) for r in range(ROWS)]
    weight = weights[0].astype(F32) * (1.0 / (2 * RING))

    own.wait()
    block = 4

    def wait_high(d):
        high[d].wait_recv()
        if d < HIGH - ROWS:
            high[ROWS + d] = send(
                window.at[LOW + ROWS + d], window.at[LOW + 2 * ROWS + d], (grid_at, below),
                high_send.at[ROWS + d], high_recv.at[ROWS + d],
            )

    def wait_low(d):
        low[d].wait_recv()
        if d < LOW - ROWS:
            low[ROWS + d] = send(
                window.at[LOW - 1 - d], window.at[LOW - 1 - ROWS - d], (grid_at, above),
                low_send.at[ROWS + d], low_recv.at[ROWS + d],
            )

    def level(d, first, stride, count, missing=None):
        m = DEGREE - d
        now, then = (held_a, held_b) if d % 2 == 0 else (held_b, held_a)

        def row(index, carry):
            r = first + index * stride
            if d > 0:
                hi, lo = split(now[r, 1 : n2 + 1].reshape(plane, n4))
                product[...] = dot(hi, t_hi[...]) + dot(lo, t_hi[...]) + dot(hi, t_lo[...])
            for i in range(0, n2, block):
                total = None
                for j in range(-d, d + 1):
                    if j == missing:
                        continue
                    term = q[m, j] * window[LOW + r + j, i : i + block]
                    total = term if total is None else total + term
                if d > 0:
                    here = now[r, i + 1 : i + 1 + block]
                    total = total + product[i * n3 : (i + block) * n3].reshape(block, n3, n4)
                    total = total + alpha[1] * now[r, i + 2 : i + 2 + block] + beta[1] * now[r, i : i + block]
                    total = total + alpha[2] * pltpu.roll(here, n3 - 1, 1) + beta[2] * pltpu.roll(here, 1, 1)
                if m > 0:
                    then[r, i + 1 : i + 1 + block] = total
                else:
                    evolved[r, i : i + block] = total
            if m > 0:
                then[r, 0] = then[r, n2]
                then[r, n2 + 1] = then[r, 1]
            return carry

        if count == 1:
            row(0, 0)
        else:
            lax.fori_loop(0, count, row, 0)

    level(0, 1, 1, 2)
    for d in range(DEGREE - 1):
        level(d, 0, 3, 2)
        level(d + 1, 1, 1, 2)
        if d > 0:
            level(d - 1, 4, 1, 1)
        wait_high(d)
        wait_low(d)
    level(DEGREE - 1, 0, 3, 2)
    level(DEGREE, 1, 1, 2)
    level(DEGREE - 2, 4, 1, 1)

    level(DEGREE, 0, 1, 1, -DEGREE)
    level(DEGREE, 3, 1, 1, DEGREE)

    def farthest(r, j):
        evolved[r] = evolved[r] + q[0, j] * window[LOW + r + j]

    def surplus_of(r, flat):
        hi, lo = split(flat)
        flat = dot(hi, fine4[...]) + dot(lo, fine4[...])
        hi, lo = split(flat)
        flat = dot(fine23[...], hi) + dot(fine23[...], lo)
        flat = flat * (mask23[...] * (weight * kept_row[r]))
        surplus[r * n2 : (r + 1) * n2] = flat.reshape(n2, n3, n4)

    def evolved_row(r):
        return evolved[r].reshape(plane, n4)

    def piece(c, h, offset):
        return pl.ds((2 * c + h) * n2 + lax.rem(z + offset + RING, RING) * part, part)

    def layer(c, h, offset, at):
        return pl.ds((2 * c + h) * n2 + lax.rem(z + offset + RING, RING) * part + at, 1)

    order = [[(0, 4), (1, 3), (0, 3), (1, 2), (0, 2), (1, 1), (0, 1)]]
    order.append([(1 - h, -o) for h, o in order[0]])
    rounds = ((0, 2, 1), (4, 3), (6, 5))
    feeds = {3: (1,), 4: (0, 2), 5: (3,), 6: (4,)}
    gorder = [[(0, 0), (1, 0), (0, -1), (1, -1), (0, -2), (1, -2), (0, -2)]]
    gorder.append([(1 - h, -o) for h, o in gorder[0]])
    grounds = ((0, 1), (2, 3), (6, 4, 5))
    inner, skip = 5, 6
    ring, ends, pairs, first, gpairs, gring, shifted = {}, {}, {}, {}, {}, {}, []

    def scatter_round(c, pace):
        for step in rounds[pace]:
            for way in range(2):
                h, offset = order[way][step]
                where = piece(c, h, offset)
                for feed in feeds.get(step, ()):
                    ring[c, way, feed].wait_recv()
                    surplus[where] = surplus[where] + arrived[c, way, feed]
                if step < inner:
                    ring[c, way, step] = send(
                        surplus.at[where], arrived.at[c, way, step], two_on[way] if step == 0 else beside[way][0],
                        ring_send.at[c, way, step], ring_recv.at[c, way, step],
                    )
                    continue
                for across, at in ((1, y_other), (0, y)):
                    ends[c, way, h, across] = send(
                        surplus.at[layer(c, h, offset, at)], last.at[c, way, h, across], beside[way][across],
                        last_send.at[c, way, h, across], last_recv.at[c, way, h, across],
                    )
        if pace == 0:
            for h in range(2):
                pairs[c, h] = send(
                    surplus.at[layer(c, h, 0, y_other)], paired.at[c, h], partner,
                    pair_send.at[c, h], pair_recv.at[c, h],
                )

    def finish(c, h):
        pairs[c, h].wait_recv()
        mine = layer(c, h, 0, y)
        total = surplus[mine] + paired[c, h]
        for across in range(2):
            for way in range(2):
                ends[c, way, h, across].wait_recv()
            total = total + (last[c, 0, h, across] + last[c, 1, h, across])
        combined[mine] = total

    def shift_row(offset):
        index = len(shifted)
        where = piece(0, 0, offset)
        target = pl.ds(ROWS * n2 + lax.rem(z + offset + RING, RING) * part, part)
        shifted.append(
            send(combined.at[where], combined.at[target], (grid_at, below), row_send.at[index], row_recv.at[index])
        )

    def landed(c, way, step):
        h, offset = gorder[way][step]
        if step < 2:
            for across in range(2):
                first[c, way, h, across].wait_recv()
        else:
            gring[c, way, step - 2].wait_recv()
        if c == 0 and h == 0:
            shift_row(offset - (1 - 2 * way) * (2 if step == skip else 1))

    def gather_round(c, pace):
        if pace == 0:
            for h in range(2):
                finish(c, h)
                mine = combined.at[layer(c, h, 0, y)]
                for across in (1, 0):
                    for way in range(2):
                        first[c, way, h, across] = send(
                            mine, mine, beside[way][across],
                            first_send.at[c, way, h, across], first_recv.at[c, way, h, across],
                        )
                gpairs[c, h] = send(mine, mine, partner, gpair_send.at[c, h], gpair_recv.at[c, h])
            return
        for step in grounds[pace]:
            for way in range(2):
                if step != 4:
                    landed(c, way, step - 2 if step < skip else 2)
                where = combined.at[piece(c, *gorder[way][step])]
                gring[c, way, step - 2] = send(
                    where, where, two_on[way] if step == skip else beside[way][0],
                    gring_send.at[c, way, step - 2], gring_recv.at[c, way, step - 2],
                )
        if pace == 1:
            for h in range(2):
                gpairs[c, h].wait_recv()
            if c == 0:
                shift_row(0)

    def gather_end(c):
        for step in (4, 5, 6):
            for way in range(2):
                landed(c, way, step)

    wait_low(DEGREE - 1)
    farthest(0, -DEGREE)
    surplus_of(0, evolved_row(0))
    surplus_of(1, evolved_row(1) - 0.5 * (evolved_row(0) + evolved_row(2)))
    scatter_round(0, 0)
    wait_high(DEGREE - 1)
    farthest(3, DEGREE)
    level(DEGREE - 1, 4, 1, 1)
    level(DEGREE, 4, 1, 1, DEGREE)
    wait_high(DEGREE)
    farthest(4, DEGREE)
    surplus_of(2, evolved_row(2) - 0.5 * (evolved_row(0) + evolved_row(4)))
    surplus_of(3, evolved_row(3) - 0.5 * (evolved_row(2) + evolved_row(4)))
    scatter_round(1, 0)
    for pace in range(1, 3):
        for c in range(2):
            scatter_round(c, pace)
    for pace in range(3):
        for c in range(2):
            gather_round(c, pace)
    gather_end(0)

    def masked(r):
        return combined[r * n2 : (r + 1) * n2].reshape(plane, n4) * mask23[...]

    def restore(r, flat):
        hi, lo = split(flat)
        flat = dot(hi, back4[...]) + dot(lo, back4[...])
        hi, lo = split(flat)
        flat = dot(back23[...], hi) + dot(back23[...], lo)
        out[0, r] = flat.reshape(n2, n3, n4)

    restore(0, masked(0))
    gather_end(1)
    for copy in shifted:
        copy.wait_recv()
    evolved[4] = masked(4).reshape(n2, n3, n4)
    evolved[2] = (kept_row[2] * masked(2) + 0.5 * (masked(0) + evolved_row(4))).reshape(n2, n3, n4)
    restore(2, evolved_row(2))
    restore(1, kept_row[1] * masked(1) + 0.5 * (masked(0) + evolved_row(2)))
    restore(3, kept_row[3] * masked(3) + 0.5 * (evolved_row(2) + evolved_row(4)))

    started = (high, low, ring, ends, pairs, first, gpairs, gring)
    for copy in (*(copy for group in started for copy in group.values()), *shifted):
        copy.wait_send()


def shards(fields, cutoffs, weights, diffusion, courant):
    n2, n3, n4 = fields.shape[2:]
    plane = n2 * n3
    part = n2 // RING
    row = (n2, n3, n4)
    dma = pltpu.SemaphoreType.DMA
    return pl.pallas_call(
        functools.partial(kernel, row),
        out_shape=jax.ShapeDtypeStruct(fields.shape, F32),
        in_specs=[pl.BlockSpec(memory_space=pltpu.SMEM)] * 4 + [pl.BlockSpec(memory_space=pl.ANY)],
        out_specs=pl.BlockSpec(memory_space=pltpu.VMEM),
        scratch_shapes=[
            pltpu.VMEM((WINDOW, *row), F32),
            pltpu.VMEM((ROWS + 1, n2 + 2, n3, n4), F32),
            pltpu.VMEM((ROWS + 1, n2 + 2, n3, n4), F32),
            pltpu.VMEM((plane, n4), F32),
            pltpu.VMEM((ROWS + 1, *row), F32),
            pltpu.VMEM((ROWS * n2, n3, n4), F32),
            pltpu.VMEM((2, 2, 5, part, n3, n4), F32),
            pltpu.VMEM((2, 2, 2, 2, 1, n3, n4), F32),
            pltpu.VMEM((2, 2, 1, n3, n4), F32),
            pltpu.VMEM(((ROWS + 1) * n2, n3, n4), F32),
            pltpu.VMEM((n4, n4), BF16),
            pltpu.VMEM((n4, n4), BF16),
            pltpu.VMEM((n4, n4), BF16),
            pltpu.VMEM((plane, plane), BF16),
            pltpu.VMEM((n4, n4), BF16),
            pltpu.VMEM((plane, plane), BF16),
            pltpu.VMEM((plane, n4), F32),
            dma, dma((LOW,)), dma((LOW,)), dma((HIGH,)), dma((HIGH,)),
            dma((2, 2, 5)), dma((2, 2, 5)), dma((2, 2, 2, 2)), dma((2, 2, 2, 2)), dma((2, 2)), dma((2, 2)),
            dma((2, 2, 2, 2)), dma((2, 2, 2, 2)), dma((2, 2)), dma((2, 2)), dma((2, 2, 5)), dma((2, 2, 5)),
            dma((8,)), dma((8,)),
        ],
        compiler_params=pltpu.CompilerParams(
            collective_id=0, has_side_effects=True, vmem_limit_bytes=52 * 1024 * 1024
        ),
        name="advect_combine",
    )(cutoffs, weights, diffusion, courant, fields)


def solution(mesh):
    in_specs = (P("grid", "dom", None, None, None), P("grid", None), P("grid"), P(), P())
    out_specs = P("grid", "dom", None, None, None)
    return jax.shard_map(shards, mesh=mesh, in_specs=in_specs, out_specs=out_specs, check_vma=False)
```

```python
import functools
import math

import jax
import jax.numpy as jnp
from jax import lax
from jax.experimental import pallas as pl
from jax.experimental.pallas import tpu as pltpu
from jax.sharding import PartitionSpec as P

SERIES = (1.0, 2.0, 2.0, 4.0 / 3.0, 7.0 / 12.0, 1.0 / 6.0, 1.0 / 36.0)
DEGREE = 6
ROWS = 4
LOW = 6
HIGH = 7
WINDOW = LOW + ROWS + HIGH
RING = 8
MESH = pl.DeviceIdType.MESH
F32 = jnp.float32
BF16 = jnp.bfloat16


def split(x):
    hi = x.astype(BF16)
    return hi, (x - hi.astype(F32)).astype(BF16)


def dot(a, b):
    return jnp.dot(a, b, preferred_element_type=F32)


def fine_surplus(to, source, n):
    ahead = (source - to) & (n - 1)
    near = (ahead == 1) | (ahead == n - 1)
    far = (ahead == 2) | (ahead == n - 2)
    half = ((to & 1) == 1) & near | ((to & 3) == 2) & far
    return jnp.where(ahead == 0, 1.0, jnp.where(half, -0.5, 0.0)).astype(F32)


def fine_restore(to, source, n):
    ahead = (source - to) & (n - 1)
    place = to & 3
    toward = jnp.where(place == 1, ahead, (n - ahead) & (n - 1))
    odd = jnp.where(
        toward == n - 1, 0.75, jnp.where(toward == 1, 0.5, jnp.where(toward == 3, 0.25, 0.0))
    )
    even = jnp.where((place == 2) & ((ahead == 2) | (ahead == n - 2)), 0.5, 0.0)
    return jnp.where(ahead == 0, 1.0, jnp.where((to & 1) == 1, odd, even)).astype(F32)


def coefficients(alpha, beta):
    up, down = [1.0], [1.0]
    for _ in range(DEGREE):
        up.append(up[-1] * alpha)
        down.append(down[-1] * beta)
    q = {}
    for m in range(DEGREE + 1):
        for j in range(m - DEGREE, DEGREE - m + 1):
            total = 0.0
            for l in range(abs(j), DEGREE - m + 1, 2):
                i = (l + j) // 2
                factor = SERIES[m + l] * math.comb(m + l, m) * math.comb(l, i)
                total = total + factor * up[i] * down[l - i]
            q[m, j] = total
    return q


def kernel(
    sizes,
    cutoffs, weights, diffusion, courant, fields, out,
    window, held_a, held_b, product, evolved, surplus, arrived, last, paired, combined,
    t_hi, t_lo, fine4, fine23, back4, back23, mask23,
    own_sem, low_send, low_recv, high_send, high_recv,
    ring_send, ring_recv, last_send, last_recv, pair_send, pair_recv,
    first_send, first_recv, gpair_send, gpair_recv, gring_send, gring_recv, row_send, row_recv,
):
    n2, n3, n4 = sizes
    plane = n2 * n3
    part = n2 // RING
    grid_at, dom_at = lax.axis_index("grid"), lax.axis_index("dom")
    doms = lax.axis_size("dom")
    above, below = lax.rem(dom_at + 1, doms), lax.rem(dom_at + doms - 1, doms)
    z = lax.rem(grid_at, RING)
    base = grid_at - z
    other = lax.rem(base + RING, 2 * RING)
    z_next = (lax.rem(z + 1, RING), lax.rem(z + RING - 1, RING))
    beside = [((base + at, dom_at), (other + at, dom_at)) for at in z_next]
    two_on = [(base + lax.rem(z + hops, RING), dom_at) for hops in (2, RING - 2)]
    partner = (other + z, dom_at)
    y = base // RING
    y_other = 1 - y

    barrier = pltpu.get_barrier_semaphore()
    for device in ((grid_at, above), (grid_at, below), *beside[0], *beside[1], *two_on, partner):
        pl.semaphore_signal(barrier, inc=1, device_id=device, device_id_type=MESH)
    own = pltpu.make_async_copy(fields.at[0], window.at[LOW : LOW + ROWS], own_sem)
    own.start()
    pl.semaphore_wait(barrier, 9)

    def send(source, target, device, send_sem, recv_sem):
        copy = pltpu.make_async_remote_copy(
            src_ref=source, dst_ref=target, send_sem=send_sem, recv_sem=recv_sem,
            device_id=device, device_id_type=MESH,
        )
        copy.start()
        return copy

    high, low = {}, {}
    for d in range(ROWS):
        high[d] = send(
            fields.at[0, d], window.at[LOW + ROWS + d], (grid_at, below), high_send.at[d], high_recv.at[d]
        )
        low[d] = send(
            fields.at[0, ROWS - 1 - d], window.at[LOW - 1 - d], (grid_at, above), low_send.at[d], low_recv.at[d]
        )
    alpha = [diffusion[d] - courant[d] for d in range(4)]
    beta = [diffusion[d] + courant[d] for d in range(4)]
    centre = -2.0 * (diffusion[0] + diffusion[1] + diffusion[2] + diffusion[3])
    q = coefficients(alpha[0], beta[0])

    source4 = lax.broadcasted_iota(jnp.int32, (n4, n4), 0)
    to4 = lax.broadcasted_iota(jnp.int32, (n4, n4), 1)
    ahead4 = (source4 - to4) & (n4 - 1)
    t = jnp.where(
        ahead4 == 0, centre, jnp.where(ahead4 == 1, alpha[3], jnp.where(ahead4 == n4 - 1, beta[3], 0.0))
    )
    hi, lo = split(t)
    t_hi[...] = hi
    t_lo[...] = lo
    fine4[...] = fine_surplus(to4, source4, n4).astype(BF16)
    back4[...] = fine_restore(to4, source4, n4).astype(BF16)
    to = lax.broadcasted_iota(jnp.int32, (plane, plane), 0)
    source = lax.broadcasted_iota(jnp.int32, (plane, plane), 1)
    shift = n3.bit_length() - 1
    to2, to3, source2, source3 = to >> shift, to & (n3 - 1), source >> shift, source & (n3 - 1)
    fine23[...] = (fine_surplus(to2, source2, n2) * fine_surplus(to3, source3, n3)).astype(BF16)
    back23[...] = (fine_restore(to2, source2, n2) * fine_restore(to3, source3, n3)).astype(BF16)
    line = lax.broadcasted_iota(jnp.int32, (plane, n4), 0)
    cell = lax.broadcasted_iota(jnp.int32, (plane, n4), 1)
    stride = [jnp.left_shift(jnp.int32(1), cutoffs[0, d]) for d in range(4)]
    off = ((line >> shift) & (stride[1] - 1)) | (line & (n3 - 1) & (stride[2] - 1)) | (cell & (stride[3] - 1))
    mask23[...] = jnp.where(off == 0, 1.0, 0.0).astype(F32)
    kept_row = [jnp.where((r & (stride[0] - 1)) == 0, 1.0, 0.0).astype(F32) for r in range(ROWS)]
    weight = weights[0].astype(F32) * (1.0 / (2 * RING))

    own.wait()
    block = 4

    def wait_high(d):
        high[d].wait_recv()
        if d < HIGH - ROWS:
            high[ROWS + d] = send(
                window.at[LOW + ROWS + d], window.at[LOW + 2 * ROWS + d], (grid_at, below),
                high_send.at[ROWS + d], high_recv.at[ROWS + d],
            )

    def wait_low(d):
        low[d].wait_recv()
        if d < LOW - ROWS:
            low[ROWS + d] = send(
                window.at[LOW - 1 - d], window.at[LOW - 1 - ROWS - d], (grid_at, above),
                low_send.at[ROWS + d], low_recv.at[ROWS + d],
            )

    def level(d, first, stride, count, missing=None):
        m = DEGREE - d
        now, then = (held_a, held_b) if d % 2 == 0 else (held_b, held_a)

        def row(index, carry):
            r = first + index * stride
            if d > 0:
                hi, lo = split(now[r, 1 : n2 + 1].reshape(plane, n4))
                product[...] = dot(hi, t_hi[...]) + dot(lo, t_hi[...]) + dot(hi, t_lo[...])
            for i in range(0, n2, block):
                total = None
                for j in range(-d, d + 1):
                    if j == missing:
                        continue
                    term = q[m, j] * window[LOW + r + j, i : i + block]
                    total = term if total is None else total + term
                if d > 0:
                    here = now[r, i + 1 : i + 1 + block]
                    total = total + product[i * n3 : (i + block) * n3].reshape(block, n3, n4)
                    total = total + alpha[1] * now[r, i + 2 : i + 2 + block] + beta[1] * now[r, i : i + block]
                    total = total + alpha[2] * pltpu.roll(here, n3 - 1, 1) + beta[2] * pltpu.roll(here, 1, 1)
                if m > 0:
                    then[r, i + 1 : i + 1 + block] = total
                else:
                    evolved[r, i : i + block] = total
            if m > 0:
                then[r, 0] = then[r, n2]
                then[r, n2 + 1] = then[r, 1]
            return carry

        if count == 1:
            row(0, 0)
        else:
            lax.fori_loop(0, count, row, 0)

    level(0, 1, 1, 2)
    for d in range(DEGREE - 1):
        level(d, 0, 3, 2)
        level(d + 1, 1, 1, 2)
        if d > 0:
            level(d - 1, 4, 1, 1)
        wait_high(d)
        wait_low(d)
    level(DEGREE - 1, 0, 1, 1)
    level(DEGREE, 1, 1, 2)

    level(DEGREE, 0, 1, 1, -DEGREE)

    def farthest(r, j):
        evolved[r] = evolved[r] + q[0, j] * window[LOW + r + j]

    def surplus_of(r, flat):
        hi, lo = split(flat)
        flat = dot(hi, fine4[...]) + dot(lo, fine4[...])
        hi, lo = split(flat)
        flat = dot(fine23[...], hi) + dot(fine23[...], lo)
        flat = flat * (mask23[...] * (weight * kept_row[r]))
        surplus[r * n2 : (r + 1) * n2] = flat.reshape(n2, n3, n4)

    def evolved_row(r):
        return evolved[r].reshape(plane, n4)

    def piece(c, h, offset):
        return pl.ds((2 * c + h) * n2 + lax.rem(z + offset + RING, RING) * part, part)

    def layer(c, h, offset, at):
        return pl.ds((2 * c + h) * n2 + lax.rem(z + offset + RING, RING) * part + at, 1)

    order = [[(0, 4), (1, 3), (0, 3), (1, 2), (0, 2), (1, 1), (0, 1)]]
    order.append([(1 - h, -o) for h, o in order[0]])
    rounds = ((0, 2, 1), (4, 3), (6, 5))
    feeds = {3: (1,), 4: (0, 2), 5: (3,), 6: (4,)}
    gorder = [[(0, 0), (1, 0), (0, -1), (1, -1), (0, -2), (1, -2), (0, -2)]]
    gorder.append([(1 - h, -o) for h, o in gorder[0]])
    grounds = ((0, 1), (2, 3), (6, 4, 5))
    inner, skip = 5, 6
    ring, ends, pairs, first, gpairs, gring, shifted = {}, {}, {}, {}, {}, {}, []

    def scatter_round(c, pace):
        for step in rounds[pace]:
            for way in range(2):
                h, offset = order[way][step]
                where = piece(c, h, offset)
                for feed in feeds.get(step, ()):
                    ring[c, way, feed].wait_recv()
                    surplus[where] = surplus[where] + arrived[c, way, feed]
                if step < inner:
                    ring[c, way, step] = send(
                        surplus.at[where], arrived.at[c, way, step], two_on[way] if step == 0 else beside[way][0],
                        ring_send.at[c, way, step], ring_recv.at[c, way, step],
                    )
                    continue
                for across, at in ((1, y_other), (0, y)):
                    ends[c, way, h, across] = send(
                        surplus.at[layer(c, h, offset, at)], last.at[c, way, h, across], beside[way][across],
                        last_send.at[c, way, h, across], last_recv.at[c, way, h, across],
                    )
        if pace == 0:
            for h in range(2):
                pairs[c, h] = send(
                    surplus.at[layer(c, h, 0, y_other)], paired.at[c, h], partner,
                    pair_send.at[c, h], pair_recv.at[c, h],
                )

    def finish(c, h):
        pairs[c, h].wait_recv()
        mine = layer(c, h, 0, y)
        total = surplus[mine] + paired[c, h]
        for across in range(2):
            for way in range(2):
                ends[c, way, h, across].wait_recv()
            total = total + (last[c, 0, h, across] + last[c, 1, h, across])
        combined[mine] = total

    def shift_row(offset):
        index = len(shifted)
        where = piece(0, 0, offset)
        target = pl.ds(ROWS * n2 + lax.rem(z + offset + RING, RING) * part, part)
        shifted.append(
            send(combined.at[where], combined.at[target], (grid_at, below), row_send.at[index], row_recv.at[index])
        )

    def landed(c, way, step):
        h, offset = gorder[way][step]
        if step < 2:
            for across in range(2):
                first[c, way, h, across].wait_recv()
        else:
            gring[c, way, step - 2].wait_recv()
        if c == 0 and h == 0:
            shift_row(offset - (1 - 2 * way) * (2 if step == skip else 1))

    def gather_round(c, pace):
        if pace == 0:
            for h in range(2):
                finish(c, h)
                mine = combined.at[layer(c, h, 0, y)]
                for across in (1, 0):
                    for way in range(2):
                        first[c, way, h, across] = send(
                            mine, mine, beside[way][across],
                            first_send.at[c, way, h, across], first_recv.at[c, way, h, across],
                        )
                gpairs[c, h] = send(mine, mine, partner, gpair_send.at[c, h], gpair_recv.at[c, h])
            return
        for step in grounds[pace]:
            for way in range(2):
                if step != 4:
                    landed(c, way, step - 2 if step < skip else 2)
                where = combined.at[piece(c, *gorder[way][step])]
                gring[c, way, step - 2] = send(
                    where, where, two_on[way] if step == skip else beside[way][0],
                    gring_send.at[c, way, step - 2], gring_recv.at[c, way, step - 2],
                )
        if pace == 1:
            for h in range(2):
                gpairs[c, h].wait_recv()
            if c == 0:
                shift_row(0)

    def gather_end(c):
        for step in (4, 5, 6):
            for way in range(2):
                landed(c, way, step)

    wait_low(DEGREE - 1)
    farthest(0, -DEGREE)
    surplus_of(0, evolved_row(0))
    surplus_of(1, evolved_row(1) - 0.5 * (evolved_row(0) + evolved_row(2)))
    scatter_round(0, 0)
    level(DEGREE - 1, 3, 1, 1)
    level(DEGREE, 3, 1, 1, DEGREE)
    level(DEGREE - 2, 4, 1, 1)
    wait_high(DEGREE - 1)
    farthest(3, DEGREE)
    level(DEGREE - 1, 4, 1, 1)
    level(DEGREE, 4, 1, 1, DEGREE)
    wait_high(DEGREE)
    farthest(4, DEGREE)
    surplus_of(2, evolved_row(2) - 0.5 * (evolved_row(0) + evolved_row(4)))
    surplus_of(3, evolved_row(3) - 0.5 * (evolved_row(2) + evolved_row(4)))
    scatter_round(1, 0)
    for pace in range(1, 3):
        for c in range(2):
            scatter_round(c, pace)
    for pace in range(3):
        for c in range(2):
            gather_round(c, pace)
    gather_end(0)

    def masked(r):
        return combined[r * n2 : (r + 1) * n2].reshape(plane, n4) * mask23[...]

    def restore(r, flat):
        hi, lo = split(flat)
        flat = dot(hi, back4[...]) + dot(lo, back4[...])
        hi, lo = split(flat)
        flat = dot(back23[...], hi) + dot(back23[...], lo)
        out[0, r] = flat.reshape(n2, n3, n4)

    restore(0, masked(0))
    gather_end(1)
    for copy in shifted:
        copy.wait_recv()
    evolved[4] = masked(4).reshape(n2, n3, n4)
    evolved[2] = (kept_row[2] * masked(2) + 0.5 * (masked(0) + evolved_row(4))).reshape(n2, n3, n4)
    restore(2, evolved_row(2))
    restore(1, kept_row[1] * masked(1) + 0.5 * (masked(0) + evolved_row(2)))
    restore(3, kept_row[3] * masked(3) + 0.5 * (evolved_row(2) + evolved_row(4)))

    started = (high, low, ring, ends, pairs, first, gpairs, gring)
    for copy in (*(copy for group in started for copy in group.values()), *shifted):
        copy.wait_send()


def shards(fields, cutoffs, weights, diffusion, courant):
    n2, n3, n4 = fields.shape[2:]
    plane = n2 * n3
    part = n2 // RING
    row = (n2, n3, n4)
    dma = pltpu.SemaphoreType.DMA
    return pl.pallas_call(
        functools.partial(kernel, row),
        out_shape=jax.ShapeDtypeStruct(fields.shape, F32),
        in_specs=[pl.BlockSpec(memory_space=pltpu.SMEM)] * 4 + [pl.BlockSpec(memory_space=pl.ANY)],
        out_specs=pl.BlockSpec(memory_space=pltpu.VMEM),
        scratch_shapes=[
            pltpu.VMEM((WINDOW, *row), F32),
            pltpu.VMEM((ROWS + 1, n2 + 2, n3, n4), F32),
            pltpu.VMEM((ROWS + 1, n2 + 2, n3, n4), F32),
            pltpu.VMEM((plane, n4), F32),
            pltpu.VMEM((ROWS + 1, *row), F32),
            pltpu.VMEM((ROWS * n2, n3, n4), F32),
            pltpu.VMEM((2, 2, 5, part, n3, n4), F32),
            pltpu.VMEM((2, 2, 2, 2, 1, n3, n4), F32),
            pltpu.VMEM((2, 2, 1, n3, n4), F32),
            pltpu.VMEM(((ROWS + 1) * n2, n3, n4), F32),
            pltpu.VMEM((n4, n4), BF16),
            pltpu.VMEM((n4, n4), BF16),
            pltpu.VMEM((n4, n4), BF16),
            pltpu.VMEM((plane, plane), BF16),
            pltpu.VMEM((n4, n4), BF16),
            pltpu.VMEM((plane, plane), BF16),
            pltpu.VMEM((plane, n4), F32),
            dma, dma((LOW,)), dma((LOW,)), dma((HIGH,)), dma((HIGH,)),
            dma((2, 2, 5)), dma((2, 2, 5)), dma((2, 2, 2, 2)), dma((2, 2, 2, 2)), dma((2, 2)), dma((2, 2)),
            dma((2, 2, 2, 2)), dma((2, 2, 2, 2)), dma((2, 2)), dma((2, 2)), dma((2, 2, 5)), dma((2, 2, 5)),
            dma((8,)), dma((8,)),
        ],
        compiler_params=pltpu.CompilerParams(
            collective_id=0, has_side_effects=True, vmem_limit_bytes=52 * 1024 * 1024
        ),
        name="advect_combine",
    )(cutoffs, weights, diffusion, courant, fields)


def solution(mesh):
    in_specs = (P("grid", "dom", None, None, None), P("grid", None), P("grid"), P(), P())
    out_specs = P("grid", "dom", None, None, None)
    return jax.shard_map(shards, mesh=mesh, in_specs=in_specs, out_specs=out_specs, check_vma=False)
```
